128 devices in a mesh: row: 16 (over z, y_lo, core), col: 8 (over x, y_hi).
Axes of the slice: x: 4, y: 4 (y_hi: 2, y_lo: 2; y = y_hi * 2 + y_lo), z: 4, core: 2. Of those that a mesh axis runs over, the one named last changes fastest.
Arguments:
- pair_in: bfloat16 [512, 512, 128], P('row', 'col'), may hold values from -6 to 6
- atoms_in: bfloat16 [12288, 128], P(('row', 'col')), may hold values from -6 to 6
- atom_token: int32 [12288], P(('row', 'col')), may hold values from 0 to 511, never falling along the last dimension, each value on 1 to 48 neighbouring positions
- atom_mask: int32 [12288], P(('row', 'col')), may hold values 0 or 1
- atom_weights: bfloat16 [5, 128, 128], replicated, may hold values from -0.5 to 0.5
- atom_trans_in: bfloat16 [2, 128, 256], replicated, may hold values from -0.5 to 0.5
- atom_trans_out: bfloat16 [256, 128], replicated, may hold values from -0.375 to 0.375
- token_in: bfloat16 [128, 384], replicated, may hold values from -0.5 to 0.5
- token_out: bfloat16 [384, 384], replicated, may hold values from -0.3125 to 0.3125
- tri_out_weights: bfloat16 [6, 128, 128], replicated, may hold values from -0.5 to 0.5
- tri_in_weights: bfloat16 [6, 128, 128], replicated, may hold values from -0.5 to 0.5
- pair_trans_in: bfloat16 [2, 128, 512], replicated, may hold values from -0.5 to 0.5
- pair_trans_out: bfloat16 [512, 128], replicated, may hold values from -0.25 to 0.25
Outputs:
- pair_out: bfloat16 [512, 512, 128], P('row', 'col')
- atoms_out: bfloat16 [12288, 128], P(('row', 'col'))
The draws below stay inside these ranges and needn't reach their ends.
Inputs may be any that keep to these rules, and one draw needn't show every extreme that they name: `atom_token`: never falls from slot to slot; every token has 1 to 48 slots, and some token exactly 48.
All inputs are finite; a program needn't handle non-finite values. No bound on the sum of `atom_mask` on one device may be relied on, other than what follows from the above.
Results may differ from the reference program's by a relative error of at most 0.015.
Values may be sent and summed in bfloat16 or wider, within the bound.
A program may use at most 128 MiB of HBM per device.

```python
import math
import jax
import jax.numpy as jnp
import numpy as np
from jax import lax

C = 128
CATOM = 128
CTOK = 384
HEADS = 4
QWIN = 32
KWIN = 128
ATOMS_TOK = 24
NTOK = 512
NATOM = 12288
NWIN = 384
SIDE = 48


def touch_ends(result, own_key, smallest, top_value):
    longest = result.shape.index(max(result.shape))
    spots = []
    for shift in (0, 1):
        where = [jax.random.randint(jax.random.fold_in(own_key, axis), (), 0, length) for axis, length in enumerate(result.shape)]
        where[longest] = (where[longest] + shift) % result.shape[longest]
        spots.append(tuple(where))
    return result.at[spots[0]].set(smallest).at[spots[1]].set(top_value)


def block_levels(rng, dims, pieces, low, top_value):
    factor_of = 1.0
    for position, shards_of in pieces:
        draws = jax.random.uniform(jax.random.fold_in(jax.random.fold_in(rng, 6), position), (shards_of,), jnp.float32, low / len(pieces), top_value / len(pieces))
        factor_of = factor_of * jnp.repeat(jnp.exp(draws), dims[position] // shards_of).reshape((-1,) + (1,) * (len(dims) - 1 - position))
    return factor_of


def split_up(number_of, total, reach, lean):
    loads = [(1 << 20) // math.isqrt(standing ** lean) + 1 for standing in range(2, number_of + 1)]
    rest, given = total - reach - (number_of - 1), [1] * (number_of - 1)
    while rest > 0:
        free = [i for i in range(number_of - 1) if given[i] < reach]
        pool, remaining = sum([loads[i] for i in free]), rest
        for i in free:
            more = min(reach - given[i], max(1, remaining * loads[i] // pool), rest)
            given[i] = given[i] + more
            rest = rest - more
    return np.array([reach] + given)


def uneven(key, amount, total, limit, slope):
    if amount == 2:
        one = jax.random.randint(key, (), max(1, total - limit), min(limit, total - 1) + 1)
        return jnp.stack([one, total - one])
    tallies = jnp.asarray(split_up(amount, total, limit, slope), jnp.int32)
    twos = (amount - 1) // 2
    giver, taker = tallies[1:1 + 2 * twos:2], tallies[2:2 + 2 * twos:2]
    slack = jnp.minimum(giver - 1, limit - taker)
    moved = jax.random.randint(jax.random.fold_in(key, 1), (twos,), 0, 1 << 20) % (slack + 1)
    tallies = tallies.at[1:1 + 2 * twos:2].set(giver - moved).at[2:2 + 2 * twos:2].set(taker + moved)
    return tallies[jax.random.permutation(jax.random.fold_in(key, 2), amount)]


def bell_draw(rng, extent, width, reach, shards=(), kind=jnp.bfloat16):
    level = block_levels(rng, extent, shards, -0.22, 0.18) if shards else 1.0
    array = jax.random.normal(rng, extent, jnp.float32) * width * level
    return jnp.minimum(jnp.maximum(array, -reach), reach).astype(kind)


def setup_inputs(seed: int = 0) -> dict:
    seeds = jax.random.split(jax.random.key(seed), 14)
    pair_in = bell_draw(seeds[0], (NTOK, NTOK, C), 1.0, 6.0, ((0, 16), (1, 8)))
    atoms_in = bell_draw(seeds[1], (NATOM, CATOM), 1.0, 6.0, ((0, 128),))
    atom_token = jnp.searchsorted(jnp.cumsum(uneven(seeds[2], NTOK, NATOM, 2 * ATOMS_TOK, 0)), jnp.arange(NATOM), side="right").astype(jnp.int32)
    atom_mask = touch_ends((jax.random.randint(seeds[3], (NATOM,), 0, 8) < 7).astype(jnp.int32), jax.random.fold_in(seeds[3], 1), 0, 1)
    atom_weights = bell_draw(seeds[4], (5, CATOM, CATOM), CATOM ** -0.5, 0.5)
    atom_trans_in = bell_draw(seeds[5], (2, CATOM, 2 * CATOM), CATOM ** -0.5, 0.5)
    atom_trans_out = bell_draw(seeds[6], (2 * CATOM, CATOM), (2 * CATOM) ** -0.5, 0.375)
    token_in = bell_draw(seeds[7], (CATOM, CTOK), CATOM ** -0.5, 0.5)
    token_out = bell_draw(seeds[8], (CTOK, 2 * C + CATOM), CTOK ** -0.5, 0.3125)
    tri_out_weights = bell_draw(seeds[9], (6, C, C), C ** -0.5, 0.5)
    tri_in_weights = bell_draw(seeds[10], (6, C, C), C ** -0.5, 0.5)
    pair_trans_in = bell_draw(seeds[11], (2, C, 4 * C), C ** -0.5, 0.5)
    pair_trans_out = bell_draw(seeds[12], (4 * C, C), (4 * C) ** -0.5, 0.25)
    return {"pair_in": pair_in, "atoms_in": atoms_in, "atom_token": atom_token, "atom_mask": atom_mask, "atom_weights": atom_weights, "atom_trans_in": atom_trans_in, "atom_trans_out": atom_trans_out, "token_in": token_in, "token_out": token_out, "tri_out_weights": tri_out_weights, "tri_in_weights": tri_in_weights, "pair_trans_in": pair_trans_in, "pair_trans_out": pair_trans_out}


epsilon = 1e-05

def layer_norm(values):
    values = values.astype(jnp.float32)
    center = values - lax.optimization_barrier(jnp.mean(values, -1, keepdims=True))
    spread = lax.optimization_barrier(jnp.mean(center * center, -1, keepdims=True))
    return center * lax.rsqrt(spread + epsilon)

def linear(inputs, weight):
    return jnp.einsum('...k,kn->...n', inputs.astype(jnp.float32), weight.astype(jnp.float32))

def edge_terms(pair_state, weights):
    normed = layer_norm(pair_state).astype(jnp.bfloat16)
    left_edge = (jax.nn.sigmoid(linear(normed, weights[0])) * linear(normed, weights[1])).astype(jnp.bfloat16)
    right_edge = (jax.nn.sigmoid(linear(normed, weights[2])) * linear(normed, weights[3])).astype(jnp.bfloat16)
    tri_gate = jax.nn.sigmoid(linear(normed, weights[4]))
    return (left_edge, right_edge, tri_gate)

def finish(pair_state, product, tri_gate, weight):
    normed = layer_norm(product).astype(jnp.bfloat16)
    return pair_state + tri_gate * linear(normed, weight)

def reference(pair_in, atoms_in, atom_token, atom_mask, atom_weights, atom_trans_in, atom_trans_out, token_in, token_out, tri_out_weights, tri_in_weights, pair_trans_in, pair_trans_out):
    atom_width = atoms_in.shape[1]
    head_dim = atom_width // HEADS
    atom_normed = layer_norm(atoms_in).astype(jnp.bfloat16)
    queries = linear(atom_normed, atom_weights[0]).astype(jnp.bfloat16)
    key_rows = linear(atom_normed, atom_weights[1]).astype(jnp.bfloat16)
    value_rows = linear(atom_normed, atom_weights[2]).astype(jnp.bfloat16)
    atom_gate = jax.nn.sigmoid(linear(atom_normed, atom_weights[3]))
    padded_keys = jnp.pad(key_rows, ((SIDE, SIDE), (0, 0)))
    padded_values = jnp.pad(value_rows, ((SIDE, SIDE), (0, 0)))
    padded_keep = jnp.pad(atom_mask, (SIDE, SIDE))
    windows = jnp.arange(NWIN, dtype=jnp.int32)
    starts = windows * QWIN - (KWIN - QWIN) // 2 + SIDE
    key_index = starts[:, None] + jnp.arange(KWIN, dtype=jnp.int32)[None, :]
    window_keys = jnp.take(padded_keys, key_index, axis=0).reshape(NWIN, KWIN, HEADS, head_dim)
    window_values = jnp.take(padded_values, key_index, axis=0).reshape(NWIN, KWIN, HEADS, head_dim)
    window_keep = jnp.take(padded_keep, key_index, axis=0)
    query_slot = windows[:, None] * QWIN + jnp.arange(QWIN, dtype=jnp.int32)[None, :]
    allowed = (window_keep[:, None, :] == 1) | ((key_index - SIDE)[:, None, :] == query_slot[:, :, None])
    window_query = queries.reshape(NWIN, QWIN, HEADS, head_dim)
    scores = jnp.einsum('wqhd,wkhd->whqk', window_query.astype(jnp.float32), window_keys.astype(jnp.float32)) * head_dim ** (-0.5)
    raw_weight = jnp.where(allowed[:, None, :, :], jnp.exp(scores), 0.0)
    attention_weights = (raw_weight / lax.optimization_barrier(jnp.sum(raw_weight, -1, keepdims=True))).astype(jnp.bfloat16)
    attended = jnp.einsum('whqk,wkhd->wqhd', attention_weights.astype(jnp.float32), window_values.astype(jnp.float32))
    attended = attended.reshape(NATOM, atom_width)
    gated = (atom_gate * attended).astype(jnp.bfloat16)
    atom_resid = atoms_in.astype(jnp.float32) + linear(gated, atom_weights[4])
    resid_normed = layer_norm(atom_resid).astype(jnp.bfloat16)
    atom_hidden = (jax.nn.silu(linear(resid_normed, atom_trans_in[0])) * linear(resid_normed, atom_trans_in[1])).astype(jnp.bfloat16)
    atom_mid = atom_resid + linear(atom_hidden, atom_trans_out)
    atom_feature = jax.nn.relu(linear(atom_mid.astype(jnp.bfloat16), token_in)).astype(jnp.bfloat16)
    live = atom_mask.astype(jnp.float32)
    token_sum = jax.ops.segment_sum(atom_feature.astype(jnp.float32) * live[:, None], atom_token, NTOK)
    token_count = jax.ops.segment_sum(live, atom_token, NTOK)
    single = (token_sum / jnp.maximum(token_count, 1.0)[:, None]).astype(jnp.bfloat16)
    token_proj = linear(single, token_out)
    pair_width = pair_in.shape[2]
    atoms_out = (atom_mid + jnp.take(token_proj[:, 2 * pair_width:], atom_token, axis=0)).astype(jnp.bfloat16)
    pair_state = pair_in.astype(jnp.float32) + token_proj[:, None, :pair_width] + token_proj[None, :, pair_width:2 * pair_width]
    left_edge, right_edge, tri_gate = edge_terms(pair_state, tri_out_weights)
    product = jnp.einsum('ikc,jkc->ijc', left_edge.astype(jnp.float32), right_edge.astype(jnp.float32))
    pair_state = finish(pair_state, product, tri_gate, tri_out_weights[5])
    left_edge, right_edge, tri_gate = edge_terms(pair_state, tri_in_weights)
    product = jnp.einsum('kic,kjc->ijc', left_edge.astype(jnp.float32), right_edge.astype(jnp.float32))
    pair_state = finish(pair_state, product, tri_gate, tri_in_weights[5])

    def transition(pair_row):
        pair_normed = layer_norm(pair_row).astype(jnp.bfloat16)
        pair_hidden = (jax.nn.silu(linear(pair_normed, pair_trans_in[0])) * linear(pair_normed, pair_trans_in[1])).astype(jnp.bfloat16)
        return (pair_row + linear(pair_hidden, pair_trans_out)).astype(jnp.bfloat16)
    pair_out = lax.map(transition, pair_state)
    return (pair_out, atoms_out)
```

```python
import jax
import jax.numpy as jnp
from jax import lax
from jax.experimental import pallas as pl
from jax.experimental.pallas import tpu as pltpu
from jax.sharding import PartitionSpec as P

HEADS = 4
QWIN = 32
KWIN = 128
SIDE = 48


epsilon = 1e-05


def with_halo(block, sides, width):
    for axis, dim in sides:
        count = lax.axis_size(axis)
        forward = [(i, i + 1) for i in range(count - 1)]
        backward = [(target, source) for source, target in forward]
        low = lax.ppermute(
            lax.slice_in_dim(block, block.shape[dim] - width, None, axis=dim), axis, forward
        )
        high = lax.ppermute(lax.slice_in_dim(block, 0, width, axis=dim), axis, backward)
        block = jnp.concatenate([low, block, high], axis=dim)
    return block


def layer_norm(values):
    values = values.astype(jnp.float32)
    center = values - jnp.mean(values, -1, keepdims=True)
    spread = jnp.mean(center * center, -1, keepdims=True)
    return center * lax.rsqrt(spread + epsilon)


def linear(inputs, weight):
    return jnp.einsum("...k,kn->...n", inputs, weight, preferred_element_type=jnp.float32)


def _peers(r, c, fn):
    for m in range(1, 128):
        n = (m * 45) % 128
        fn(lax.rem(r + n // 8, 16), lax.rem(c + n % 8, 8))


def _sigmoid(x):
    return 0.5 * jnp.tanh(0.5 * x) + 0.5


def _norm(x):
    center = x - jnp.mean(x, 0, keepdims=True)
    spread = jnp.mean(center * center, 0, keepdims=True)
    return center * lax.rsqrt(spread + epsilon)


def _dot(a, b):
    return jnp.dot(a, b, preferred_element_type=jnp.float32)


def _flip(x):
    return jnp.transpose(x.astype(jnp.float32)).astype(jnp.bfloat16)


def _pair_kernel(
    pair_ref, left_ref, right_ref, out_w_ref, in_w_ref, tin_ref, tout_ref, result_ref,
    state, normed, gate, rows32, weights, tin_t, tout_t,
    send_l, send_r, send_p, recv_l, recv_r, recv_p, mat_l, mat_r, mat_p, wide,
    sent, got, entered,
):
    r = lax.axis_index("row")
    c = lax.axis_index("col")
    me = r * 8 + c
    barrier = pltpu.get_barrier_semaphore()

    def greet(semaphore, row, col):
        pl.semaphore_signal(
            semaphore, inc=1, device_id=(row, col), device_id_type=pl.DeviceIdType.MESH
        )

    for step in range(1, 8):
        greet(barrier, r, lax.rem(c + step, 8))
    for step in range(1, 16):
        greet(barrier, lax.rem(r + step, 16), c)

    for w in range(6):
        weights[pl.ds(w * 128, 128), :] = _flip(out_w_ref[w])
        weights[pl.ds((6 + w) * 128, 128), :] = _flip(in_w_ref[w])
    for w in range(2):
        tin_t[pl.ds(w * 512, 512), :] = _flip(tin_ref[w])
    tout_t[...] = _flip(tout_ref[...])

    def start_state(a, _):
        natural = jnp.concatenate([pair_ref[a], pair_ref[a + 16]], 0).astype(jnp.float32)
        right = right_ref[...]
        natural = natural + jnp.concatenate(
            [right + left_ref[pl.ds(a, 1), :], right + left_ref[pl.ds(a + 16, 1), :]], 0
        )
        turned = jnp.transpose(natural)
        state[a] = turned
        normed[a] = _norm(turned).astype(jnp.bfloat16)
        return 0

    lax.fori_loop(0, 16, start_state, 0)

    pl.semaphore_wait(barrier, 22)
    for step in range(1, 16):
        greet(entered, lax.rem(r + step, 16), c)
    pl.semaphore_wait(entered, 15)

    def pack(target):
        def move(d, _):
            target[pl.ds(d * 8, 8)] = (
                rows32[pl.ds(d * 128, 128), :].reshape(8, 16, 128).astype(jnp.bfloat16)
            )
            return 0

        lax.fori_loop(0, 16, move, 0)

    def launch(source, target, k):
        target[me] = source[me]

        def one(row, col):
            pltpu.make_async_remote_copy(
                src_ref=source.at[row * 8 + col],
                dst_ref=target.at[me],
                send_sem=sent.at[k],
                recv_sem=got.at[k],
                device_id=(row, col),
                device_id_type=pl.DeviceIdType.MESH,
            ).start()

        _peers(r, c, one)

    def finish_copies(source, target, k):
        part = pl.ds(0, 127)
        pltpu.make_async_copy(source.at[part], source.at[part], sent.at[k]).wait()
        pltpu.make_async_copy(target.at[part], target.at[part], got.at[k]).wait()

    def edges(base, first):
        def chunk(a, _):
            both = _dot(weights[pl.ds((base + first) * 128, 256), :], normed[a])
            rows32[pl.ds(a, 128, stride=16), :] = _sigmoid(both[:128]) * both[128:]
            return 0

        lax.fori_loop(0, 16, chunk, 0)

    def gates(base):
        def chunk(a, _):
            gate[a] = _sigmoid(_dot(weights[pl.ds((base + 4) * 128, 128), :], normed[a]))
            return 0

        lax.fori_loop(0, 16, chunk, 0)

    def assemble(source, target):
        def block(row, _):
            for q in range(4):
                even = source[row * 8 + 2 * q]
                odd = source[row * 8 + 2 * q + 1]
                target[pl.ds(row * 32, 16), pl.ds(q * 128, 128)] = jnp.concatenate(
                    [even[:, :64], odd[:, :64]], 1
                )
                target[pl.ds(row * 32 + 16, 16), pl.ds(q * 128, 128)] = jnp.concatenate(
                    [even[:, 64:], odd[:, 64:]], 1
                )
            return 0

        lax.fori_loop(0, 16, block, 0)

    def split(source, target):
        def block(row, _):
            for q in range(4):
                top = source[pl.ds(row * 32, 16), pl.ds(q * 128, 128)]
                low = source[pl.ds(row * 32 + 16, 16), pl.ds(q * 128, 128)]
                target[row * 8 + 2 * q] = jnp.concatenate([top[:, :64], low[:, :64]], 1)
                target[row * 8 + 2 * q + 1] = jnp.concatenate([top[:, 64:], low[:, 64:]], 1)
            return 0

        lax.fori_loop(0, 16, block, 0)

    def triangle(t, after):
        base = 6 * t
        edges(base, 0)
        pack(send_l.at[t])
        launch(send_l.at[t], recv_l.at[t], 3 * t)
        edges(base, 2)
        pack(send_r.at[t])
        launch(send_r.at[t], recv_r.at[t], 3 * t + 1)
        gates(base)
        finish_copies(send_l.at[t], recv_l.at[t], 3 * t)
        assemble(recv_l.at[t], mat_l)
        finish_copies(send_r.at[t], recv_r.at[t], 3 * t + 1)
        assemble(recv_r.at[t], mat_r)
        axis = 1 - t
        mat_p[...] = lax.dot_general(
            mat_l[...],
            mat_r[...],
            (((axis,), (axis,)), ((), ())),
            preferred_element_type=jnp.float32,
        ).astype(jnp.bfloat16)
        split(mat_p, send_p.at[t])
        launch(send_p.at[t], recv_p.at[t], 3 * t + 2)
        finish_copies(send_p.at[t], recv_p.at[t], 3 * t + 2)

        def widen(d, _):
            rows32[pl.ds(d * 128, 128), :] = (
                recv_p[t, pl.ds(d * 8, 8)].astype(jnp.float32).reshape(128, 128)
            )
            return 0

        lax.fori_loop(0, 16, widen, 0)

        def close(a, _):
            product = _norm(rows32[pl.ds(a, 128, stride=16), :]).astype(jnp.bfloat16)
            updated = state[a] + gate[a] * _dot(weights[pl.ds((base + 5) * 128, 128), :], product)
            state[a] = updated
            normed[a] = _norm(updated).astype(jnp.bfloat16)
            if after is not None:
                after(a, updated)
            return 0

        lax.fori_loop(0, 16, close, 0)

    def transition(a, updated):
        inner = _dot(tin_t[...], normed[a])
        up = inner[:512]
        hidden = (up * _sigmoid(up) * inner[512:]).astype(jnp.bfloat16)
        final = jnp.transpose(updated + _dot(tout_t[...], hidden)).astype(jnp.bfloat16)
        result_ref[a] = final[:64]
        result_ref[a + 16] = final[64:]

    triangle(0, None)
    triangle(1, transition)


def _pair_trunk(pair_in, left_add, right_add, out_w, in_w, tin, tout):
    vmem = pl.BlockSpec(memory_space=pltpu.VMEM)
    message = (2, 128, 16, 128)
    return pl.pallas_call(
        _pair_kernel,
        out_shape=jax.ShapeDtypeStruct(pair_in.shape, jnp.bfloat16),
        in_specs=[vmem] * 7,
        out_specs=vmem,
        scratch_shapes=[
            pltpu.VMEM((16, 128, 128), jnp.float32),
            pltpu.VMEM((16, 128, 128), jnp.bfloat16),
            pltpu.VMEM((16, 128, 128), jnp.float32),
            pltpu.VMEM((2048, 128), jnp.float32),
            pltpu.VMEM((1536, 128), jnp.bfloat16),
            pltpu.VMEM((1024, 128), jnp.bfloat16),
            pltpu.VMEM((128, 512), jnp.bfloat16),
        ]
        + [pltpu.VMEM(message, jnp.bfloat16)] * 6
        + [pltpu.VMEM((512, 512), jnp.bfloat16)] * 3
        + [
            pltpu.VMEM((8, 128), jnp.float32),
            pltpu.SemaphoreType.DMA((6,)),
            pltpu.SemaphoreType.DMA((6,)),
            pltpu.SemaphoreType.REGULAR,
        ],
        compiler_params=pltpu.CompilerParams(
            collective_id=0, has_side_effects=True, vmem_limit_bytes=48 * 1024 * 1024
        ),
        name="pair_trunk",
    )(pair_in, left_add, right_add, out_w, in_w, tin, tout)


def project_keys(normed, atom_weights):
    return jnp.concatenate(
        [linear(normed, atom_weights[1]), linear(normed, atom_weights[2])], 1
    ).astype(jnp.bfloat16)


def attend(queries, wide_kv, wide_keep):
    slot_count, atom_width = queries.shape
    window_count = slot_count // QWIN
    head_dim = atom_width // HEADS
    starts = jnp.arange(window_count, dtype=jnp.int32) * QWIN - (KWIN - QWIN) // 2 + SIDE
    key_index = starts[:, None] + jnp.arange(KWIN, dtype=jnp.int32)[None, :]
    window_kv = jnp.take(wide_kv, key_index, axis=0)
    window_keep = jnp.take(wide_keep, key_index, axis=0)
    query_slot = jnp.arange(slot_count, dtype=jnp.int32).reshape(window_count, QWIN)
    allowed = (window_keep[:, None, :] > 0) | (
        (key_index - SIDE)[:, None, :] == query_slot[:, :, None]
    )
    window_query = queries.reshape(window_count, QWIN, HEADS, head_dim)
    window_keys = window_kv[..., :atom_width].reshape(window_count, KWIN, HEADS, head_dim)
    window_values = window_kv[..., atom_width:].reshape(window_count, KWIN, HEADS, head_dim)
    scores = jnp.einsum(
        "wqhd,wkhd->whqk", window_query, window_keys, preferred_element_type=jnp.float32
    ) * head_dim ** (-0.5)
    raw_weight = jnp.where(allowed[:, None, :, :], jnp.exp(scores), 0.0)
    attention_weights = (raw_weight / jnp.sum(raw_weight, -1, keepdims=True)).astype(jnp.bfloat16)
    attended = jnp.einsum(
        "whqk,wkhd->wqhd", attention_weights, window_values, preferred_element_type=jnp.float32
    )
    return attended.reshape(slot_count, atom_width)


def body(
    pair_in,
    atoms_in,
    atom_token,
    atom_mask,
    atom_weights,
    atom_trans_in,
    atom_trans_out,
    token_in,
    token_out,
    tri_out_weights,
    tri_in_weights,
    pair_trans_in,
    pair_trans_out,
):
    atom_normed = layer_norm(atoms_in).astype(jnp.bfloat16)
    queries = linear(atom_normed, atom_weights[0]).astype(jnp.bfloat16)
    atom_gate = jax.nn.sigmoid(linear(atom_normed, atom_weights[3]))
    keep_flags = atom_mask.astype(jnp.bfloat16)
    key_values = project_keys(atom_normed, atom_weights)
    wide_kv, wide_keep = (
        with_halo(key_values, ((("row", "col"), 0),), SIDE),
        with_halo(keep_flags, ((("row", "col"), 0),), SIDE),
    )
    attended = attend(queries, wide_kv, wide_keep)
    gated = (atom_gate * attended).astype(jnp.bfloat16)
    atom_resid = atoms_in.astype(jnp.float32) + linear(gated, atom_weights[4])
    resid_normed = layer_norm(atom_resid).astype(jnp.bfloat16)
    atom_hidden = (
        jax.nn.silu(linear(resid_normed, atom_trans_in[0])) * linear(resid_normed, atom_trans_in[1])
    ).astype(jnp.bfloat16)
    atom_mid = atom_resid + linear(atom_hidden, atom_trans_out)
    atom_feature = jax.nn.relu(linear(atom_mid.astype(jnp.bfloat16), token_in)).astype(jnp.bfloat16)
    row_tokens, col_tokens, pair_width = pair_in.shape
    token_total = row_tokens * lax.axis_size("row")
    member = (atom_token[None, :] == jnp.arange(token_total, dtype=jnp.int32)[:, None]) & (
        atom_mask[None, :] == 1
    )
    partial_sums = jnp.dot(
        member.astype(jnp.bfloat16), atom_feature, preferred_element_type=jnp.float32
    )
    partial_counts = jnp.sum(member.astype(jnp.float32), 1)
    token_sums, token_counts = lax.psum((partial_sums, partial_counts), ("row", "col"))
    single = (token_sums / jnp.maximum(token_counts, 1.0)[:, None]).astype(jnp.bfloat16)
    token_proj = jnp.dot(single, token_out, preferred_element_type=jnp.float32)
    atoms_out = (atom_mid + jnp.take(token_proj[:, 2 * pair_width :], atom_token, axis=0)).astype(
        jnp.bfloat16
    )
    row_index = lax.axis_index("row")
    col_index = lax.axis_index("col")
    left_add = lax.dynamic_slice_in_dim(
        token_proj[:, :pair_width], row_index * row_tokens, row_tokens, 0
    )
    right_add = lax.dynamic_slice_in_dim(
        token_proj[:, pair_width : 2 * pair_width], col_index * col_tokens, col_tokens, 0
    )
    pair_out = _pair_trunk(
        pair_in,
        left_add,
        right_add,
        tri_out_weights,
        tri_in_weights,
        pair_trans_in,
        pair_trans_out,
    )
    return (pair_out, atoms_out)


def solution(mesh):
    placed = (
        P("row", "col", None),
        P(("row", "col"), None),
        P(("row", "col")),
        P(("row", "col")),
        P(),
        P(),
        P(),
        P(),
        P(),
        P(),
        P(),
        P(),
        P(),
    )
    return jax.shard_map(
        body,
        mesh=mesh,
        in_specs=placed,
        out_specs=(P("row", "col", None), P(("row", "col"), None)),
        check_vma=False,
    )
```

```python
import jax
import jax.numpy as jnp
from jax import lax
from jax.experimental import pallas as pl
from jax.experimental.pallas import tpu as pltpu
from jax.sharding import PartitionSpec as P

HEADS = 4
QWIN = 32
KWIN = 128
SIDE = 48
SLOTS = 96
WIDE = SLOTS + 2 * SIDE

epsilon = 1e-05

def _peers(r, c, fn):
    for m in range(1, 128):
        n = (m * 45) % 128
        fn(lax.rem(r + n // 8, 16), lax.rem(c + n % 8, 8))


def _sigmoid(x):
    return 0.5 * jnp.tanh(0.5 * x) + 0.5


def _norm(x):
    center = x - jnp.mean(x, 0, keepdims=True)
    spread = jnp.mean(center * center, 0, keepdims=True)
    return center * lax.rsqrt(spread + epsilon)


def _dot(a, b):
    return jnp.dot(a, b, preferred_element_type=jnp.float32)


def _flip(x):
    return jnp.transpose(x.astype(jnp.float32)).astype(jnp.bfloat16)


def _norm_rows(x):
    center = x - jnp.mean(x, -1, keepdims=True)
    spread = jnp.mean(center * center, -1, keepdims=True)
    return center * lax.rsqrt(spread + epsilon)


def _ones_where(condition):
    return jnp.where(condition, 1.0, 0.0).astype(jnp.bfloat16)


def _kernel(
    pair_ref, atoms_ref, token_ref, mask_ref, atom_w_ref, atom_tin_ref, atom_tout_ref,
    token_in_ref, token_out_ref, out_w_ref, in_w_ref, tin_ref, tout_ref,
    result_ref, atoms_out_ref,
    state, normed, gate, rows32, weights, tin_t, tout_t,
    send_l, send_r, send_p, recv_l, recv_r, recv_p, mat_l, mat_r, mat_p,
    halo_out, halo_in, flags, live_token, any_token, wide, mid, featured,
    send_t, recv_t, share, recv_row, recv_right, left32, right64, add32, recv_add,
    sent, got, entered,
):
    r = lax.axis_index("row")
    c = lax.axis_index("col")
    me = r * 8 + c
    barrier = pltpu.get_barrier_semaphore()
    after = lax.rem(me + 1, 128)
    before = lax.rem(me + 127, 128)

    def greet(semaphore, row, col):
        pl.semaphore_signal(
            semaphore, inc=1, device_id=(row, col), device_id_type=pl.DeviceIdType.MESH
        )

    def copy(source, target, k, row, col):
        pltpu.make_async_remote_copy(
            src_ref=source,
            dst_ref=target,
            send_sem=sent.at[k],
            recv_sem=got.at[k],
            device_id=(row, col),
            device_id_type=pl.DeviceIdType.MESH,
        ).start()

    def await_bytes(ref, semaphore):
        pltpu.make_async_copy(ref, ref, semaphore).wait()

    greet(barrier, after // 8, lax.rem(after, 8))
    greet(barrier, before // 8, lax.rem(before, 8))
    for step in range(1, 8):
        greet(barrier, r, lax.rem(c + step, 8))
    for step in range(1, 16):
        greet(barrier, lax.rem(r + step, 16), c)

    flags[...] = jnp.zeros_like(flags)
    flags[:, :SLOTS] = jnp.broadcast_to(
        jnp.where(mask_ref[...] == 1, 1.0, 0.0), (16, SLOTS)
    )
    any_token[...] = jnp.full_like(any_token, -1)
    any_token[:, :SLOTS] = jnp.broadcast_to(token_ref[...], (8, SLOTS))
    own_flags = flags[...].astype(jnp.bfloat16)
    halo_out[0, :SIDE] = atoms_ref[SLOTS - SIDE :]
    halo_out[1, :SIDE] = atoms_ref[:SIDE]
    halo_out[0, SIDE:] = own_flags
    halo_out[1, SIDE:] = own_flags
    live_token[...] = jnp.where(flags[:8] > 0.5, any_token[...], -1)
    pl.semaphore_wait(barrier, 24)
    copy(halo_out.at[0], halo_in.at[0], 6, after // 8, lax.rem(after, 8))
    copy(halo_out.at[1], halo_in.at[1], 7, before // 8, lax.rem(before, 8))
    for step in range(1, 16):
        greet(entered, lax.rem(r + step, 16), c)

    for w in range(6):
        weights[pl.ds(w * 128, 128), :] = _flip(out_w_ref[w])
        weights[pl.ds((6 + w) * 128, 128), :] = _flip(in_w_ref[w])
    for w in range(2):
        tin_t[pl.ds(w * 512, 512), :] = _flip(tin_ref[w])
    tout_t[...] = _flip(tout_ref[...])

    own = atoms_ref[...].astype(jnp.float32)
    own_normed = _norm_rows(own).astype(jnp.bfloat16)
    wide[SIDE : SIDE + SLOTS] = own_normed
    queries = _dot(own_normed, atom_w_ref[0]).astype(jnp.bfloat16)
    atom_gate = _sigmoid(_dot(own_normed, atom_w_ref[3]))
    for k in (6, 7):
        await_bytes(halo_out.at[k - 6], sent.at[k])
        await_bytes(halo_in.at[k - 6], got.at[k])
    wide[:SIDE] = _norm_rows(halo_in[0, :SIDE].astype(jnp.float32)).astype(jnp.bfloat16)
    wide[SIDE + SLOTS :] = _norm_rows(halo_in[1, :SIDE].astype(jnp.float32)).astype(jnp.bfloat16)
    keys = _dot(wide[...], atom_w_ref[1]).astype(jnp.bfloat16)
    values = _dot(wide[...], atom_w_ref[2]).astype(jnp.bfloat16)
    slot = lax.broadcasted_iota(jnp.int32, (128, WIDE), 0)
    key = lax.broadcasted_iota(jnp.int32, (128, WIDE), 1)
    keep = (
        _dot(halo_in[0, SIDE:], _ones_where((key + SIDE == slot) & (me > 0)))
        + _dot(own_flags, _ones_where(key - SIDE == slot))
        + _dot(halo_in[1, SIDE:], _ones_where((key - SIDE - SLOTS == slot) & (me < 127)))
    )[:1]
    query = lax.broadcasted_iota(jnp.int32, (SLOTS, WIDE), 0)
    key = lax.broadcasted_iota(jnp.int32, (SLOTS, WIDE), 1)
    offset = key - (query // QWIN) * QWIN
    inside = (offset >= 0) & (offset < KWIN)
    allowed = jnp.where(inside & ((keep > 0.5) | (key - SIDE == query)), 1.0, 0.0)
    lane_head = lax.broadcasted_iota(jnp.int32, (SLOTS, 128), 1) // 32
    stacked = jnp.concatenate(
        [jnp.where(lane_head == h, queries.astype(jnp.float32), 0.0) for h in range(HEADS)], 0
    ).astype(jnp.bfloat16)
    scores = (
        lax.dot_general(
            stacked, keys, (((1,), (1,)), ((), ())), preferred_element_type=jnp.float32
        )
        * 32**-0.5
    )
    raw = jnp.where(jnp.concatenate([allowed] * HEADS, 0) > 0.5, jnp.exp(scores), 0.0)
    attention = (raw / jnp.sum(raw, -1, keepdims=True)).astype(jnp.bfloat16)
    spread = _dot(attention, values)
    attended = jnp.zeros((SLOTS, 128), jnp.float32)
    for h in range(HEADS):
        attended = attended + jnp.where(lane_head == h, spread[h * SLOTS : (h + 1) * SLOTS], 0.0)
    gated = (atom_gate * attended).astype(jnp.bfloat16)
    resid = own + _dot(gated, atom_w_ref[4])
    resid_normed = _norm_rows(resid).astype(jnp.bfloat16)
    up = _dot(resid_normed, atom_tin_ref[0])
    hidden = (up * _sigmoid(up) * _dot(resid_normed, atom_tin_ref[1])).astype(jnp.bfloat16)
    atom_mid = resid + _dot(hidden, atom_tout_ref[...])
    mid[...] = atom_mid
    feature = jnp.maximum(_dot(atom_mid.astype(jnp.bfloat16), token_in_ref[...]), 0.0)
    featured[...] = jnp.zeros_like(featured)
    featured[:SLOTS, :384] = feature.astype(jnp.bfloat16)
    featured[:SLOTS, 384:] = jnp.ones((SLOTS, 128), jnp.bfloat16)

    for t in range(4):
        owner = lax.broadcasted_iota(jnp.int32, (128, 128), 0)
        member = _ones_where(owner * 4 + t == live_token[:1])
        sums = _dot(member, featured[...])
        for m in range(4):
            rows32[pl.ds(4 * m + t, 128, stride=16), :] = sums[:, m * 128 : (m + 1) * 128]

    def pack(target):
        def move(d, _):
            target[pl.ds(d * 8, 8)] = (
                rows32[pl.ds(d * 128, 128), :].reshape(8, 16, 128).astype(jnp.bfloat16)
            )
            return 0

        lax.fori_loop(0, 16, move, 0)

    def launch(source, target, k):
        target[me] = source[me]
        _peers(r, c, lambda row, col: copy(source.at[row * 8 + col], target.at[me], k, row, col))

    def finish_copies(source, target, k):
        part = pl.ds(0, 127)
        await_bytes(source.at[part], sent.at[k])
        await_bytes(target.at[part], got.at[k])

    pack(send_t)
    pl.semaphore_wait(entered, 15)
    launch(send_t, recv_t, 8)
    finish_copies(send_t, recv_t, 8)

    def gather_sums(d, total):
        return total + jnp.sum(recv_t[pl.ds(d * 8, 8)].astype(jnp.float32), 0)

    total = lax.fori_loop(0, 16, gather_sums, jnp.zeros((16, 128), jnp.float32))
    count = jnp.maximum(total[12:], 1.0)
    proj = jnp.zeros((4, 384), jnp.float32)
    for m in range(3):
        single = (total[4 * m : 4 * m + 4] / count).astype(jnp.bfloat16)
        proj = proj + _dot(single, token_out_ref[pl.ds(m * 128, 128), :])
    share[...] = jnp.zeros_like(share)
    for m in range(3):
        share[4 * m : 4 * m + 4] = proj[:, m * 128 : (m + 1) * 128]

    recv_row[c] = share[...]
    column = me // 16
    place = lax.rem(me, 16)
    for step in range(1, 8):
        copy(share, recv_row.at[c], 9, r, lax.rem(c + step, 8))
    for step in range(1, 16):
        row = lax.rem(r + step, 16)
        copy(share.at[pl.ds(0, 8)], recv_right.at[place], 10, row, column)

    @pl.when(column == c)
    def _():
        recv_right[place] = share[pl.ds(0, 8)]

    @pl.when(column != c)
    def _():
        copy(share.at[pl.ds(0, 8)], recv_right.at[place], 10, r, column)
        await_bytes(recv_right.at[pl.ds(0, 1)], sent.at[10])
    await_bytes(recv_right.at[pl.ds(0, 15)], sent.at[10])
    await_bytes(recv_row.at[pl.ds(0, 7)], sent.at[9])

    mine = (me >= 16 * c) & (me < 16 * c + 16)

    @pl.when(mine)
    def _():
        await_bytes(recv_right.at[pl.ds(0, 15)], got.at[10])

    @pl.when(jnp.logical_not(mine))
    def _():
        await_bytes(recv_right, got.at[10])

    await_bytes(recv_row.at[pl.ds(0, 7)], got.at[9])
    for j in range(16):
        right64[4 * j : 4 * j + 4] = recv_right[j, 4:8]
    for j in range(8):
        left32[4 * j : 4 * j + 4] = recv_row[j, :4]
        add32[4 * j : 4 * j + 4] = recv_row[j, 8:12]
    recv_add[r] = add32[...]
    for step in range(1, 16):
        copy(add32, recv_add.at[r], 11, lax.rem(r + step, 16), c)

    def start_state(a, _):
        natural = jnp.concatenate([pair_ref[a], pair_ref[a + 16]], 0).astype(jnp.float32)
        right = right64[...]
        natural = natural + jnp.concatenate(
            [right + left32[pl.ds(a, 1), :], right + left32[pl.ds(a + 16, 1), :]], 0
        )
        turned = jnp.transpose(natural)
        state[a] = turned
        normed[a] = _norm(turned).astype(jnp.bfloat16)
        return 0

    lax.fori_loop(0, 16, start_state, 0)

    def edges(base, first):
        def chunk(a, _):
            both = _dot(weights[pl.ds((base + first) * 128, 256), :], normed[a])
            rows32[pl.ds(a, 128, stride=16), :] = _sigmoid(both[:128]) * both[128:]
            return 0

        lax.fori_loop(0, 16, chunk, 0)

    def gates(base):
        def chunk(a, _):
            gate[a] = _sigmoid(_dot(weights[pl.ds((base + 4) * 128, 128), :], normed[a]))
            return 0

        lax.fori_loop(0, 16, chunk, 0)

    def assemble(source, target):
        def block(row, _):
            for q in range(4):
                even = source[row * 8 + 2 * q]
                odd = source[row * 8 + 2 * q + 1]
                target[pl.ds(row * 32, 16), pl.ds(q * 128, 128)] = jnp.concatenate(
                    [even[:, :64], odd[:, :64]], 1
                )
                target[pl.ds(row * 32 + 16, 16), pl.ds(q * 128, 128)] = jnp.concatenate(
                    [even[:, 64:], odd[:, 64:]], 1
                )
            return 0

        lax.fori_loop(0, 16, block, 0)

    def split(source, target):
        def block(row, _):
            for q in range(4):
                top = source[pl.ds(row * 32, 16), pl.ds(q * 128, 128)]
                low = source[pl.ds(row * 32 + 16, 16), pl.ds(q * 128, 128)]
                target[row * 8 + 2 * q] = jnp.concatenate([top[:, :64], low[:, :64]], 1)
                target[row * 8 + 2 * q + 1] = jnp.concatenate([top[:, 64:], low[:, 64:]], 1)
            return 0

        lax.fori_loop(0, 16, block, 0)

    def triangle(t, after):
        base = 6 * t
        edges(base, 0)
        pack(send_l.at[t])
        launch(send_l.at[t], recv_l.at[t], 3 * t)
        edges(base, 2)
        pack(send_r.at[t])
        launch(send_r.at[t], recv_r.at[t], 3 * t + 1)
        gates(base)
        finish_copies(send_l.at[t], recv_l.at[t], 3 * t)
        assemble(recv_l.at[t], mat_l)
        finish_copies(send_r.at[t], recv_r.at[t], 3 * t + 1)
        assemble(recv_r.at[t], mat_r)
        axis = 1 - t
        mat_p[...] = lax.dot_general(
            mat_l[...],
            mat_r[...],
            (((axis,), (axis,)), ((), ())),
            preferred_element_type=jnp.float32,
        ).astype(jnp.bfloat16)
        split(mat_p, send_p.at[t])
        launch(send_p.at[t], recv_p.at[t], 3 * t + 2)
        finish_copies(send_p.at[t], recv_p.at[t], 3 * t + 2)

        def widen(d, _):
            rows32[pl.ds(d * 128, 128), :] = (
                recv_p[t, pl.ds(d * 8, 8)].astype(jnp.float32).reshape(128, 128)
            )
            return 0

        lax.fori_loop(0, 16, widen, 0)

        def close(a, _):
            product = _norm(rows32[pl.ds(a, 128, stride=16), :]).astype(jnp.bfloat16)
            updated = state[a] + gate[a] * _dot(weights[pl.ds((base + 5) * 128, 128), :], product)
            state[a] = updated
            normed[a] = _norm(updated).astype(jnp.bfloat16)
            if after is not None:
                after(a, updated)
            return 0

        lax.fori_loop(0, 16, close, 0)

    def transition(a, updated):
        inner = _dot(tin_t[...], normed[a])
        up = inner[:512]
        hidden = (up * _sigmoid(up) * inner[512:]).astype(jnp.bfloat16)
        final = jnp.transpose(updated + _dot(tout_t[...], hidden)).astype(jnp.bfloat16)
        result_ref[a] = final[:64]
        result_ref[a + 16] = final[64:]

    triangle(0, None)
    triangle(1, transition)

    await_bytes(recv_add.at[pl.ds(0, 15)], sent.at[11])
    await_bytes(recv_add.at[pl.ds(0, 15)], got.at[11])
    added = recv_add[...].reshape(512, 128)
    high = added.astype(jnp.bfloat16)
    low = (added - high.astype(jnp.float32)).astype(jnp.bfloat16)
    token = lax.broadcasted_iota(jnp.int32, (512, 128), 0)
    chosen = _ones_where(token == any_token[:1])
    over = (((0,), (0,)), ((), ()))
    picked = lax.dot_general(
        chosen, high, over, preferred_element_type=jnp.float32
    ) + lax.dot_general(chosen, low, over, preferred_element_type=jnp.float32)
    atoms_out_ref[...] = (mid[...] + picked[:SLOTS]).astype(jnp.bfloat16)


def body(pair_in, atoms_in, atom_token, atom_mask, *parameters):
    vmem = pl.BlockSpec(memory_space=pltpu.VMEM)
    bf16, f32 = jnp.bfloat16, jnp.float32
    message = (2, 128, 16, 128)
    return pl.pallas_call(
        _kernel,
        out_shape=(
            jax.ShapeDtypeStruct(pair_in.shape, bf16),
            jax.ShapeDtypeStruct(atoms_in.shape, bf16),
        ),
        in_specs=[vmem] * 13,
        out_specs=(vmem, vmem),
        scratch_shapes=[
            pltpu.VMEM((16, 128, 128), f32),
            pltpu.VMEM((16, 128, 128), bf16),
            pltpu.VMEM((16, 128, 128), f32),
            pltpu.VMEM((2048, 128), f32),
            pltpu.VMEM((1536, 128), bf16),
            pltpu.VMEM((1024, 128), bf16),
            pltpu.VMEM((128, 512), bf16),
        ]
        + [pltpu.VMEM(message, bf16)] * 6
        + [pltpu.VMEM((512, 512), bf16)] * 3
        + [
            pltpu.VMEM((2, 64, 128), bf16),
            pltpu.VMEM((2, 64, 128), bf16),
            pltpu.VMEM((16, 128), f32),
            pltpu.VMEM((8, 128), jnp.int32),
            pltpu.VMEM((8, 128), jnp.int32),
            pltpu.VMEM((WIDE, 128), bf16),
            pltpu.VMEM((SLOTS, 128), f32),
            pltpu.VMEM((128, 512), bf16),
            pltpu.VMEM((128, 16, 128), bf16),
            pltpu.VMEM((128, 16, 128), bf16),
            pltpu.VMEM((16, 128), f32),
            pltpu.VMEM((8, 16, 128), f32),
            pltpu.VMEM((16, 8, 128), f32),
            pltpu.VMEM((32, 128), f32),
            pltpu.VMEM((64, 128), f32),
            pltpu.VMEM((32, 128), f32),
            pltpu.VMEM((16, 32, 128), f32),
            pltpu.SemaphoreType.DMA((12,)),
            pltpu.SemaphoreType.DMA((12,)),
            pltpu.SemaphoreType.REGULAR,
        ],
        compiler_params=pltpu.CompilerParams(
            collective_id=0, has_side_effects=True, vmem_limit_bytes=48 * 1024 * 1024
        ),
        name="atoms_and_pair",
    )(pair_in, atoms_in, atom_token.reshape(1, SLOTS), atom_mask.reshape(1, SLOTS), *parameters)


def solution(mesh):
    placed = (
        P("row", "col", None),
        P(("row", "col"), None),
        P(("row", "col")),
        P(("row", "col")),
        P(),
        P(),
        P(),
        P(),
        P(),
        P(),
        P(),
        P(),
        P(),
    )
    return jax.shard_map(
        body,
        mesh=mesh,
        in_specs=placed,
        out_specs=(P("row", "col", None), P(("row", "col"), None)),
        check_vma=False,
    )
```

```python
import jax
import jax.numpy as jnp
from jax import lax
from jax.experimental import pallas as pl
from jax.experimental.pallas import tpu as pltpu
from jax.sharding import PartitionSpec as P

HEADS = 4
QWIN = 32
KWIN = 128
SIDE = 48
SLOTS = 96
WIDE = SLOTS + 2 * SIDE
START = 512
EDGE = 2048
CLOSE = 512
LAST = 1024
ROWS = 16

epsilon = 1e-05

def _far_first():
    shifts = [
        (x, y, z, core) for x in range(4) for y in range(4) for z in range(4) for core in range(2)
    ][1:]
    return sorted(shifts, key=lambda shift: -sum(min(s, 4 - s) for s in shift[:3]))


def _peers(r, c):
    z, y, core, x = r // 4, lax.rem(c, 2) * 2 + lax.rem(r // 2, 2), lax.rem(r, 2), c // 2
    col_x = [lax.rem(x + s, 4) * 2 for s in range(4)]
    ys = [lax.rem(y + s, 4) for s in range(4)]
    col_y = [s // 2 for s in ys]
    row_y = [lax.rem(s, 2) * 2 for s in ys]
    row_z = [lax.rem(z + s, 4) * 4 for s in range(4)]
    cores = [core, 1 - core]
    return [
        (row_z[dz] + row_y[dy] + cores[dcore], col_x[dx] + col_y[dy])
        for dx, dy, dz, dcore in _far_first()
    ]


def _sigmoid(x):
    return 0.5 * jnp.tanh(0.5 * x) + 0.5


def _norm(x):
    center = x - jnp.mean(x, 0, keepdims=True)
    spread = jnp.mean(center * center, 0, keepdims=True)
    return center * lax.rsqrt(spread + epsilon)


def _dot(a, b):
    return jnp.dot(a, b, preferred_element_type=jnp.float32)


def _flip(x):
    return jnp.transpose(x.astype(jnp.float32)).astype(jnp.bfloat16)


def _norm_rows(x):
    center = x - jnp.mean(x, -1, keepdims=True)
    spread = jnp.mean(center * center, -1, keepdims=True)
    return center * lax.rsqrt(spread + epsilon)


def _ones_where(condition):
    return jnp.where(condition, 1.0, 0.0).astype(jnp.bfloat16)


def _kernel(
    token_ref, mask_ref, *refs,
):
    sources, refs = refs[:11], refs[11:]
    result_ref, atoms_out_ref, *refs = refs
    staged, refs = refs[:11], refs[11:]
    (pair_ref, atoms_ref, atom_w_ref, atom_tin_ref, atom_tout_ref,
     token_in_ref, token_out_ref, out_w_ref, in_w_ref, tin_ref, tout_ref) = staged
    (    state, normed, gate, rows32, weights, tin_t, tout_t,
    send_l, send_r, send_p, recv_l, recv_r, recv_p, mat_l, mat_r, mat_p,
    halo_out, halo_in, flags, live_token, any_token, wide, mid, featured,
    send_t, recv_t, share, recv_row, recv_right, left32, right64, add32, recv_add,
    sent, got, entered, loaded) = refs
    r = lax.axis_index("row")
    c = lax.axis_index("col")
    me = r * 8 + c
    peers = _peers(r, c)
    barrier = pltpu.get_barrier_semaphore()
    after = lax.rem(me + 1, 128)
    before = lax.rem(me + 127, 128)

    def greet(semaphore, row, col):
        pl.semaphore_signal(
            semaphore, inc=1, device_id=(row, col), device_id_type=pl.DeviceIdType.MESH
        )

    def copy(source, target, k, row, col):
        pltpu.make_async_remote_copy(
            src_ref=source,
            dst_ref=target,
            send_sem=sent.at[k],
            recv_sem=got.at[k],
            device_id=(row, col),
            device_id_type=pl.DeviceIdType.MESH,
        ).start()

    def await_bytes(ref, semaphore):
        pltpu.make_async_copy(ref, ref, semaphore).wait()

    greet(barrier, after // 8, lax.rem(after, 8))
    greet(barrier, before // 8, lax.rem(before, 8))
    for step in range(1, 8):
        greet(barrier, r, lax.rem(c + step, 8))
    for step in range(1, 16):
        greet(barrier, lax.rem(r + step, 16), c)

    loads = [
        pltpu.make_async_copy(source, place, loaded.at[k])
        for k, (source, place) in enumerate(zip(sources, staged))
    ]
    for k in (1, 2, 3, 4, 5, 6, 0, 7, 8, 9, 10):
        loads[k].start()

    flags[...] = jnp.zeros_like(flags)
    flags[:, :SLOTS] = jnp.broadcast_to(
        jnp.where(mask_ref[...] == 1, 1.0, 0.0), (16, SLOTS)
    )
    any_token[...] = jnp.full_like(any_token, -1)
    any_token[:, :SLOTS] = jnp.broadcast_to(token_ref[...], (8, SLOTS))
    own_flags = flags[...].astype(jnp.bfloat16)
    loads[1].wait()
    halo_out[0, :SIDE] = atoms_ref[SLOTS - SIDE :]
    halo_out[1, :SIDE] = atoms_ref[:SIDE]
    halo_out[0, SIDE:] = own_flags
    halo_out[1, SIDE:] = own_flags
    live_token[...] = jnp.where(flags[:8] > 0.5, any_token[...], -1)
    pl.semaphore_wait(barrier, 24)
    copy(halo_out.at[0], halo_in.at[0], 6, after // 8, lax.rem(after, 8))
    copy(halo_out.at[1], halo_in.at[1], 7, before // 8, lax.rem(before, 8))
    for step in range(1, 16):
        greet(entered, lax.rem(r + step, 16), c)

    for k in range(7, 11):
        loads[k].wait()
    for w in range(6):
        weights[pl.ds(w * 128, 128), :] = _flip(out_w_ref[w])
        weights[pl.ds((6 + w) * 128, 128), :] = _flip(in_w_ref[w])
    for w in range(2):
        tin_t[pl.ds(w * 512, 512), :] = _flip(tin_ref[w])
    tout_t[...] = _flip(tout_ref[...])

    own = atoms_ref[...].astype(jnp.float32)
    own_normed = _norm_rows(own).astype(jnp.bfloat16)
    wide[SIDE : SIDE + SLOTS] = own_normed
    loads[2].wait()
    queries = _dot(own_normed, atom_w_ref[0]).astype(jnp.bfloat16)
    atom_gate = _sigmoid(_dot(own_normed, atom_w_ref[3]))
    for k in (6, 7):
        await_bytes(halo_out.at[k - 6], sent.at[k])
        await_bytes(halo_in.at[k - 6], got.at[k])
    wide[:SIDE] = _norm_rows(halo_in[0, :SIDE].astype(jnp.float32)).astype(jnp.bfloat16)
    wide[SIDE + SLOTS :] = _norm_rows(halo_in[1, :SIDE].astype(jnp.float32)).astype(jnp.bfloat16)
    keys = _dot(wide[...], atom_w_ref[1]).astype(jnp.bfloat16)
    values = _dot(wide[...], atom_w_ref[2]).astype(jnp.bfloat16)
    slot = lax.broadcasted_iota(jnp.int32, (128, WIDE), 0)
    key = lax.broadcasted_iota(jnp.int32, (128, WIDE), 1)
    keep = (
        _dot(halo_in[0, SIDE:], _ones_where((key + SIDE == slot) & (me > 0)))
        + _dot(own_flags, _ones_where(key - SIDE == slot))
        + _dot(halo_in[1, SIDE:], _ones_where((key - SIDE - SLOTS == slot) & (me < 127)))
    )[:1]
    query = lax.broadcasted_iota(jnp.int32, (SLOTS, WIDE), 0)
    key = lax.broadcasted_iota(jnp.int32, (SLOTS, WIDE), 1)
    offset = key - (query // QWIN) * QWIN
    inside = (offset >= 0) & (offset < KWIN)
    allowed = jnp.where(inside & ((keep > 0.5) | (key - SIDE == query)), 1.0, 0.0)
    lane_head = lax.broadcasted_iota(jnp.int32, (SLOTS, 128), 1) // 32
    stacked = jnp.concatenate(
        [jnp.where(lane_head == h, queries.astype(jnp.float32), 0.0) for h in range(HEADS)], 0
    ).astype(jnp.bfloat16)
    scores = (
        lax.dot_general(
            stacked, keys, (((1,), (1,)), ((), ())), preferred_element_type=jnp.float32
        )
        * 32**-0.5
    )
    raw = jnp.where(jnp.concatenate([allowed] * HEADS, 0) > 0.5, jnp.exp(scores), 0.0)
    attention = (raw / jnp.sum(raw, -1, keepdims=True)).astype(jnp.bfloat16)
    spread = _dot(attention, values)
    attended = jnp.zeros((SLOTS, 128), jnp.float32)
    for h in range(HEADS):
        attended = attended + jnp.where(lane_head == h, spread[h * SLOTS : (h + 1) * SLOTS], 0.0)
    gated = (atom_gate * attended).astype(jnp.bfloat16)
    resid = own + _dot(gated, atom_w_ref[4])
    resid_normed = _norm_rows(resid).astype(jnp.bfloat16)
    for k in (3, 4, 5):
        loads[k].wait()
    up = _dot(resid_normed, atom_tin_ref[0])
    hidden = (up * _sigmoid(up) * _dot(resid_normed, atom_tin_ref[1])).astype(jnp.bfloat16)
    atom_mid = resid + _dot(hidden, atom_tout_ref[...])
    mid[...] = atom_mid
    feature = jnp.maximum(_dot(atom_mid.astype(jnp.bfloat16), token_in_ref[...]), 0.0)
    featured[...] = jnp.zeros_like(featured)
    featured[:SLOTS, :384] = feature.astype(jnp.bfloat16)
    featured[:SLOTS, 384:] = jnp.ones((SLOTS, 128), jnp.bfloat16)

    for t in range(4):
        owner = lax.broadcasted_iota(jnp.int32, (128, 128), 0)
        member = _ones_where(owner * 4 + t == live_token[:1])
        sums = _dot(member, featured[...])
        for m in range(4):
            rows32[pl.ds(4 * m + t, 128, stride=16), :] = sums[:, m * 128 : (m + 1) * 128]

    def pack(target):
        def move(d, _):
            target[pl.ds(d * 8, 8)] = (
                rows32[pl.ds(d * 128, 128), :].reshape(8, 16, 128).astype(jnp.bfloat16)
            )
            return 0

        lax.fori_loop(0, 16, move, 0)

    def launch(source, target, k):
        target[me] = source[me]
        for row, col in peers:
            copy(source.at[row * 8 + col], target.at[me], k, row, col)

    def finish_copies(source, target, k):
        part = pl.ds(0, 127)
        await_bytes(source.at[part], sent.at[k])
        await_bytes(target.at[part], got.at[k])

    pack(send_t)
    pl.semaphore_wait(entered, 15)
    launch(send_t, recv_t, 8)
    finish_copies(send_t, recv_t, 8)

    def gather_sums(d, total):
        return total + jnp.sum(recv_t[pl.ds(d * 8, 8)].astype(jnp.float32), 0)

    total = lax.fori_loop(0, 16, gather_sums, jnp.zeros((16, 128), jnp.float32))
    loads[6].wait()
    count = jnp.maximum(total[12:], 1.0)
    proj = jnp.zeros((4, 384), jnp.float32)
    for m in range(3):
        single = (total[4 * m : 4 * m + 4] / count).astype(jnp.bfloat16)
        proj = proj + _dot(single, token_out_ref[pl.ds(m * 128, 128), :])
    share[...] = jnp.zeros_like(share)
    for m in range(3):
        share[4 * m : 4 * m + 4] = proj[:, m * 128 : (m + 1) * 128]

    recv_row[c] = share[...]
    column = me // 16
    place = lax.rem(me, 16)
    for step in range(1, 8):
        copy(share, recv_row.at[c], 9, r, lax.rem(c + step, 8))
    for step in range(1, 16):
        row = lax.rem(r + step, 16)
        copy(share.at[pl.ds(0, 8)], recv_right.at[place], 10, row, column)

    @pl.when(column == c)
    def _():
        recv_right[place] = share[pl.ds(0, 8)]

    @pl.when(column != c)
    def _():
        copy(share.at[pl.ds(0, 8)], recv_right.at[place], 10, r, column)
        await_bytes(recv_right.at[pl.ds(0, 1)], sent.at[10])
    await_bytes(recv_right.at[pl.ds(0, 15)], sent.at[10])
    await_bytes(recv_row.at[pl.ds(0, 7)], sent.at[9])

    mine = (me >= 16 * c) & (me < 16 * c + 16)

    @pl.when(mine)
    def _():
        await_bytes(recv_right.at[pl.ds(0, 15)], got.at[10])

    @pl.when(jnp.logical_not(mine))
    def _():
        await_bytes(recv_right, got.at[10])

    await_bytes(recv_row.at[pl.ds(0, 7)], got.at[9])
    for j in range(16):
        right64[4 * j : 4 * j + 4] = recv_right[j, 4:8]
    for j in range(8):
        left32[4 * j : 4 * j + 4] = recv_row[j, :4]
        add32[4 * j : 4 * j + 4] = recv_row[j, 8:12]
    recv_add[r] = add32[...]
    for step in range(1, 16):
        copy(add32, recv_add.at[r], 11, lax.rem(r + step, 16), c)

    loads[0].wait()

    def spans(width, step):
        if width == 2048:
            step(0)
        else:
            lax.fori_loop(0, 2048 // width, lambda g, _: (step(g), 0)[1], 0)

    def lanes(g, width):
        return pl.ds(g * width if isinstance(g, int) else pl.multiple_of(g * width, width), width)

    def start_state(g):
        right = right64[...]
        for h in range(START // 128):
            a = g * (START // 128) + h
            natural = jnp.concatenate([pair_ref[a], pair_ref[a + 16]], 0).astype(jnp.float32)
            natural = natural + jnp.concatenate(
                [right + left32[pl.ds(a, 1), :], right + left32[pl.ds(a + 16, 1), :]], 0
            )
            turned = jnp.transpose(natural)
            state[:, lanes(a, 128)] = turned
            normed[:, lanes(a, 128)] = _norm(turned).astype(jnp.bfloat16)

    spans(START, start_state)

    def edges(base, first):
        def chunk(g):
            both = _dot(weights[pl.ds((base + first) * 128, 256), :], normed[:, lanes(g, EDGE)])
            edge = _sigmoid(both[:128]) * both[128:]
            for h in range(EDGE // 128):
                rows32[pl.ds(g * (EDGE // 128) + h, 128, stride=16), :] = edge[
                    :, h * 128 : (h + 1) * 128
                ]

        spans(EDGE, chunk)

    def gates(base):
        def chunk(g):
            gate[:, lanes(g, EDGE)] = _sigmoid(
                _dot(weights[pl.ds((base + 4) * 128, 128), :], normed[:, lanes(g, EDGE)])
            )

        spans(EDGE, chunk)

    low_lanes = lax.broadcasted_iota(jnp.int32, (16, 128), 1) < 64

    def assemble(source, target):
        def block(g, _):
            for k in range(ROWS):
                row = g * ROWS + k
                for q in range(4):
                    even = source[row * 8 + 2 * q]
                    odd = source[row * 8 + 2 * q + 1]
                    target[pl.ds(row * 32, 16), pl.ds(q * 128, 128)] = jnp.where(
                        low_lanes, even, pltpu.roll(odd, 64, 1)
                    )
                    target[pl.ds(row * 32 + 16, 16), pl.ds(q * 128, 128)] = jnp.where(
                        low_lanes, pltpu.roll(even, 64, 1), odd
                    )
            return 0

        lax.fori_loop(0, 16 // ROWS, block, 0)

    def split(source, target):
        def block(g, _):
            for k in range(ROWS):
                row = g * ROWS + k
                for q in range(4):
                    top = source[pl.ds(row * 32, 16), pl.ds(q * 128, 128)]
                    low = source[pl.ds(row * 32 + 16, 16), pl.ds(q * 128, 128)]
                    target[row * 8 + 2 * q] = jnp.where(low_lanes, top, pltpu.roll(low, 64, 1))
                    target[row * 8 + 2 * q + 1] = jnp.where(low_lanes, pltpu.roll(top, 64, 1), low)
            return 0

        lax.fori_loop(0, 16 // ROWS, block, 0)

    def triangle(t, width, after):
        base = 6 * t
        edges(base, 0)
        pack(send_l.at[t])
        launch(send_l.at[t], recv_l.at[t], 3 * t)
        edges(base, 2)
        pack(send_r.at[t])
        launch(send_r.at[t], recv_r.at[t], 3 * t + 1)
        gates(base)
        finish_copies(send_l.at[t], recv_l.at[t], 3 * t)
        assemble(recv_l.at[t], mat_l)
        finish_copies(send_r.at[t], recv_r.at[t], 3 * t + 1)
        assemble(recv_r.at[t], mat_r)
        axis = 1 - t
        mat_p[...] = lax.dot_general(
            mat_l[...],
            mat_r[...],
            (((axis,), (axis,)), ((), ())),
            preferred_element_type=jnp.float32,
        ).astype(jnp.bfloat16)
        split(mat_p, send_p.at[t])
        launch(send_p.at[t], recv_p.at[t], 3 * t + 2)
        finish_copies(send_p.at[t], recv_p.at[t], 3 * t + 2)

        def widen(d, _):
            rows32[pl.ds(d * 128, 128), :] = (
                recv_p[t, pl.ds(d * 8, 8)].astype(jnp.float32).reshape(128, 128)
            )
            return 0

        lax.fori_loop(0, 16, widen, 0)

        def close(g):
            count = width // 128
            product = jnp.concatenate(
                [rows32[pl.ds(g * count + h, 128, stride=16), :] for h in range(count)], 1
            )
            product = _norm(product).astype(jnp.bfloat16)
            here = lanes(g, width)
            updated = state[:, here] + gate[:, here] * _dot(
                weights[pl.ds((base + 5) * 128, 128), :], product
            )
            after(g, width, updated)

        spans(width, close)

    def next_update(g, width, updated):
        state[:, lanes(g, width)] = updated
        normed[:, lanes(g, width)] = _norm(updated).astype(jnp.bfloat16)

    def transition(g, width, updated):
        inner = _dot(tin_t[...], _norm(updated).astype(jnp.bfloat16))
        up = inner[:512]
        hidden = (up * _sigmoid(up) * inner[512:]).astype(jnp.bfloat16)
        final = updated + _dot(tout_t[...], hidden)
        for h in range(width // 128):
            natural = jnp.transpose(final[:, h * 128 : (h + 1) * 128]).astype(jnp.bfloat16)
            result_ref[g * (width // 128) + h] = natural[:64]
            result_ref[g * (width // 128) + h + 16] = natural[64:]

    triangle(0, CLOSE, next_update)
    triangle(1, LAST, transition)

    await_bytes(recv_add.at[pl.ds(0, 15)], sent.at[11])
    await_bytes(recv_add.at[pl.ds(0, 15)], got.at[11])
    added = recv_add[...].reshape(512, 128)
    high = added.astype(jnp.bfloat16)
    low = (added - high.astype(jnp.float32)).astype(jnp.bfloat16)
    token = lax.broadcasted_iota(jnp.int32, (512, 128), 0)
    chosen = _ones_where(token == any_token[:1])
    over = (((0,), (0,)), ((), ()))
    picked = lax.dot_general(
        chosen, high, over, preferred_element_type=jnp.float32
    ) + lax.dot_general(chosen, low, over, preferred_element_type=jnp.float32)
    atoms_out_ref[...] = (mid[...] + picked[:SLOTS]).astype(jnp.bfloat16)


def body(pair_in, atoms_in, atom_token, atom_mask, *parameters):
    vmem = pl.BlockSpec(memory_space=pltpu.VMEM)
    staged = (pair_in, atoms_in, *parameters)
    bf16, f32 = jnp.bfloat16, jnp.float32
    message = (2, 128, 16, 128)
    return pl.pallas_call(
        _kernel,
        out_shape=(
            jax.ShapeDtypeStruct(pair_in.shape, bf16),
            jax.ShapeDtypeStruct(atoms_in.shape, bf16),
        ),
        in_specs=[vmem] * 2 + [pl.BlockSpec(memory_space=pltpu.HBM)] * 11,
        out_specs=(vmem, vmem),
        scratch_shapes=[pltpu.VMEM(array.shape, array.dtype) for array in staged]
        + [
            pltpu.VMEM((128, 2048), f32),
            pltpu.VMEM((128, 2048), bf16),
            pltpu.VMEM((128, 2048), f32),
            pltpu.VMEM((2048, 128), f32),
            pltpu.VMEM((1536, 128), bf16),
            pltpu.VMEM((1024, 128), bf16),
            pltpu.VMEM((128, 512), bf16),
        ]
        + [pltpu.VMEM(message, bf16)] * 6
        + [pltpu.VMEM((512, 512), bf16)] * 3
        + [
            pltpu.VMEM((2, 64, 128), bf16),
            pltpu.VMEM((2, 64, 128), bf16),
            pltpu.VMEM((16, 128), f32),
            pltpu.VMEM((8, 128), jnp.int32),
            pltpu.VMEM((8, 128), jnp.int32),
            pltpu.VMEM((WIDE, 128), bf16),
            pltpu.VMEM((SLOTS, 128), f32),
            pltpu.VMEM((128, 512), bf16),
            pltpu.VMEM((128, 16, 128), bf16),
            pltpu.VMEM((128, 16, 128), bf16),
            pltpu.VMEM((16, 128), f32),
            pltpu.VMEM((8, 16, 128), f32),
            pltpu.VMEM((16, 8, 128), f32),
            pltpu.VMEM((32, 128), f32),
            pltpu.VMEM((64, 128), f32),
            pltpu.VMEM((32, 128), f32),
            pltpu.VMEM((16, 32, 128), f32),
            pltpu.SemaphoreType.DMA((12,)),
            pltpu.SemaphoreType.DMA((12,)),
            pltpu.SemaphoreType.REGULAR,
            pltpu.SemaphoreType.DMA((11,)),
        ],
        compiler_params=pltpu.CompilerParams(
            collective_id=0, has_side_effects=True, vmem_limit_bytes=60 * 1024 * 1024
        ),
        name="atoms_and_pair",
    )(atom_token.reshape(1, SLOTS), atom_mask.reshape(1, SLOTS), *staged)


def solution(mesh):
    placed = (
        P("row", "col", None),
        P(("row", "col"), None),
        P(("row", "col")),
        P(("row", "col")),
        P(),
        P(),
        P(),
        P(),
        P(),
        P(),
        P(),
        P(),
        P(),
    )
    return jax.shard_map(
        body,
        mesh=mesh,
        in_specs=placed,
        out_specs=(P("row", "col", None), P(("row", "col"), None)),
        check_vma=False,
    )
```

```python
import jax
import jax.numpy as jnp
from jax import lax
from jax.experimental import pallas as pl
from jax.experimental.pallas import tpu as pltpu
from jax.sharding import PartitionSpec as P

HEADS = 4
QWIN = 32
KWIN = 128
SIDE = 48
SLOTS = 96
WIDE = SLOTS + 2 * SIDE
START = 2048
EDGE = 2048
CLOSE = 2048
LAST = 1024
ROWS = 16

epsilon = 1e-05

def _far_first():
    shifts = [(x, y, z) for x in range(4) for y in range(4) for z in range(4)][1:]
    return sorted(shifts, key=lambda shift: -sum(min(s, 4 - s) for s in shift))


def _chips(r, c):
    z, y, x = r // 4, lax.rem(c, 2) * 2 + lax.rem(r // 2, 2), c // 2
    xs, ys, zs = [[lax.rem(v + s, 4) for s in range(4)] for v in (x, y, z)]
    row_y = [lax.rem(v, 2) * 2 for v in ys]
    col_y = [v // 2 for v in ys]

    def chip(dx, dy, dz):
        row = zs[dz] * 4 + row_y[dy]
        return row, xs[dx] * 2 + col_y[dy], xs[dx] * 8 + ys[dy] * 2 + zs[dz] // 2

    others = [chip(*shift) + (sum(shift) % 2,) for shift in _far_first()]
    return chip(0, 0, 0)[2], lax.rem(x + y + z, 2), others


def _sigmoid(x):
    return 0.5 * jnp.tanh(0.5 * x) + 0.5


def _norm(x):
    center = x - jnp.mean(x, 0, keepdims=True)
    spread = jnp.mean(center * center, 0, keepdims=True)
    return center * lax.rsqrt(spread + epsilon)


def _dot(a, b):
    return jnp.dot(a, b, preferred_element_type=jnp.float32)


def _flip(x):
    return jnp.transpose(x.astype(jnp.float32)).astype(jnp.bfloat16)


def _norm_rows(x):
    center = x - jnp.mean(x, -1, keepdims=True)
    spread = jnp.mean(center * center, -1, keepdims=True)
    return center * lax.rsqrt(spread + epsilon)


def _ones_where(condition):
    return jnp.where(condition, 1.0, 0.0).astype(jnp.bfloat16)


def _kernel(
    token_ref, mask_ref, *refs,
):
    sources, refs = refs[:11], refs[11:]
    result_ref, atoms_out_ref, *refs = refs
    staged, refs = refs[:11], refs[11:]
    (pair_ref, atoms_ref, atom_w_ref, atom_tin_ref, atom_tout_ref,
     token_in_ref, token_out_ref, out_w_ref, in_w_ref, tin_ref, tout_ref) = staged
    (    state, normed, gate, rows32, weights, tin_t, tout_t,
    send_e, recv_e, edge32, send_p, recv_p, mat_l, mat_r, mat_p,
    halo_out, halo_in, flags, live_token, any_token, wide, mid, featured,
    send_t, recv_t, share, recv_row, recv_right, spreader, add32, recv_add,
    sent, got, entered, loaded) = refs
    r = lax.axis_index("row")
    c = lax.axis_index("col")
    me = r * 8 + c
    spot, parity, chips = _chips(r, c)
    core = lax.rem(r, 2)
    sibling = r + 1 - 2 * core
    channel = core * 64 + parity * 32 + spot
    sibling_channel = (1 - core) * 64 + parity * 32 + spot
    barrier = pltpu.get_barrier_semaphore()
    after = lax.rem(me + 1, 128)
    before = lax.rem(me + 127, 128)

    def greet(semaphore, row, col):
        pl.semaphore_signal(
            semaphore, inc=1, device_id=(row, col), device_id_type=pl.DeviceIdType.MESH
        )

    def copy(source, target, k, row, col):
        pltpu.make_async_remote_copy(
            src_ref=source,
            dst_ref=target,
            send_sem=sent.at[k],
            recv_sem=got.at[k],
            device_id=(row, col),
            device_id_type=pl.DeviceIdType.MESH,
        ).start()

    def await_bytes(ref, semaphore):
        pltpu.make_async_copy(ref, ref, semaphore).wait()

    greet(barrier, after // 8, lax.rem(after, 8))
    greet(barrier, before // 8, lax.rem(before, 8))
    for step in range(1, 8):
        greet(barrier, r, lax.rem(c + step, 8))
    for step in range(1, 16):
        greet(barrier, lax.rem(r + step, 16), c)

    loads = [
        pltpu.make_async_copy(source, place, loaded.at[k])
        for k, (source, place) in enumerate(zip(sources, staged))
    ]
    for k in (1, 2, 3, 4, 5, 6, 0, 7, 8, 9, 10):
        loads[k].start()

    flags[...] = jnp.zeros_like(flags)
    flags[:, :SLOTS] = jnp.broadcast_to(
        jnp.where(mask_ref[...] == 1, 1.0, 0.0), (16, SLOTS)
    )
    featured[0] = jnp.zeros((128, 512), jnp.bfloat16)
    featured[0, :SLOTS, 384:] = jnp.ones((SLOTS, 128), jnp.bfloat16)
    any_token[...] = jnp.full_like(any_token, -1)
    any_token[:, :SLOTS] = jnp.broadcast_to(token_ref[...], (8, SLOTS))
    own_flags = flags[...].astype(jnp.bfloat16)
    loads[1].wait()
    halo_out[0, :SIDE] = atoms_ref[SLOTS - SIDE :]
    halo_out[1, :SIDE] = atoms_ref[:SIDE]
    halo_out[0, SIDE:] = own_flags
    halo_out[1, SIDE:] = own_flags
    live_token[0] = jnp.where(flags[:8] > 0.5, any_token[...], -1)
    pl.semaphore_wait(barrier, 24)
    copy(halo_out.at[0], halo_in.at[0], 6, after // 8, lax.rem(after, 8))
    copy(halo_out.at[1], halo_in.at[1], 7, before // 8, lax.rem(before, 8))
    for step in range(1, 16):
        greet(entered, lax.rem(r + step, 16), c)

    own = atoms_ref[...].astype(jnp.float32)
    own_normed = _norm_rows(own).astype(jnp.bfloat16)
    wide[SIDE : SIDE + SLOTS] = own_normed
    loads[2].wait()
    queries = _dot(own_normed, atom_w_ref[0]).astype(jnp.bfloat16)
    atom_gate = _sigmoid(_dot(own_normed, atom_w_ref[3]))
    for k in (6, 7):
        await_bytes(halo_out.at[k - 6], sent.at[k])
        await_bytes(halo_in.at[k - 6], got.at[k])
    wide[:SIDE] = _norm_rows(halo_in[0, :SIDE].astype(jnp.float32)).astype(jnp.bfloat16)
    wide[SIDE + SLOTS :] = _norm_rows(halo_in[1, :SIDE].astype(jnp.float32)).astype(jnp.bfloat16)
    keys = _dot(wide[...], atom_w_ref[1]).astype(jnp.bfloat16)
    values = _dot(wide[...], atom_w_ref[2]).astype(jnp.bfloat16)
    slot = lax.broadcasted_iota(jnp.int32, (128, WIDE), 0)
    key = lax.broadcasted_iota(jnp.int32, (128, WIDE), 1)
    keep = (
        _dot(halo_in[0, SIDE:], _ones_where((key + SIDE == slot) & (me > 0)))
        + _dot(own_flags, _ones_where(key - SIDE == slot))
        + _dot(halo_in[1, SIDE:], _ones_where((key - SIDE - SLOTS == slot) & (me < 127)))
    )[:1]
    query = lax.broadcasted_iota(jnp.int32, (SLOTS, WIDE), 0)
    key = lax.broadcasted_iota(jnp.int32, (SLOTS, WIDE), 1)
    offset = key - (query // QWIN) * QWIN
    inside = (offset >= 0) & (offset < KWIN)
    allowed = jnp.where(inside & ((keep > 0.5) | (key - SIDE == query)), 1.0, 0.0)
    lane_head = lax.broadcasted_iota(jnp.int32, (SLOTS, 128), 1) // 32
    stacked = jnp.concatenate(
        [jnp.where(lane_head == h, queries.astype(jnp.float32), 0.0) for h in range(HEADS)], 0
    ).astype(jnp.bfloat16)
    scores = (
        lax.dot_general(
            stacked, keys, (((1,), (1,)), ((), ())), preferred_element_type=jnp.float32
        )
        * 32**-0.5
    )
    raw = jnp.where(jnp.concatenate([allowed] * HEADS, 0) > 0.5, jnp.exp(scores), 0.0)
    attention = (raw / jnp.sum(raw, -1, keepdims=True)).astype(jnp.bfloat16)
    spread = _dot(attention, values)
    attended = jnp.zeros((SLOTS, 128), jnp.float32)
    for h in range(HEADS):
        attended = attended + jnp.where(lane_head == h, spread[h * SLOTS : (h + 1) * SLOTS], 0.0)
    gated = (atom_gate * attended).astype(jnp.bfloat16)
    resid = own + _dot(gated, atom_w_ref[4])
    resid_normed = _norm_rows(resid).astype(jnp.bfloat16)
    for k in (3, 4, 5):
        loads[k].wait()
    up = _dot(resid_normed, atom_tin_ref[0])
    hidden = (up * _sigmoid(up) * _dot(resid_normed, atom_tin_ref[1])).astype(jnp.bfloat16)
    atom_mid = resid + _dot(hidden, atom_tout_ref[...])
    mid[...] = atom_mid
    feature = jnp.maximum(_dot(atom_mid.astype(jnp.bfloat16), token_in_ref[...]), 0.0)
    featured[0, :SLOTS, :384] = feature.astype(jnp.bfloat16)
    copy(featured.at[0], featured.at[1], 8, sibling, c)
    copy(live_token.at[0], live_token.at[1], 9, sibling, c)

    await_bytes(featured.at[0], sent.at[8])
    await_bytes(live_token.at[0], sent.at[9])
    await_bytes(featured.at[1], got.at[8])
    await_bytes(live_token.at[1], got.at[9])
    slots_token = jnp.concatenate([live_token[0, :1], live_token[1, :1]], 1)
    both = featured[...].reshape(256, 512)
    place = lax.broadcasted_iota(jnp.int32, (64, 256), 0)
    owner = place // 8 * 16 + core * 8 + place % 8
    for t in range(4):
        sums = _dot(_ones_where(owner * 4 + t == slots_token), both)
        for m in range(4):
            rows32[pl.ds(4 * m + t, 64, stride=16), :] = sums[:, m * 128 : (m + 1) * 128]

    def pack(target, first, count):
        target[first : first + count] = (
            rows32[first * 16 : (first + count) * 16].reshape(count, 16, 128).astype(jnp.bfloat16)
        )

    def launch(source, target, k, slot):
        target[slot] = source[me]
        for row, col, _, _ in chips:
            copy(source.at[row * 8 + col], target.at[slot], k, row, col)
            copy(source.at[row * 8 + 8 + col], target.at[slot], k, row + 1, col)
        copy(source.at[sibling * 8 + c], target.at[slot], k, sibling, c)

    def launch_quarter(source, target, k, half, turn):
        first = half * 64 + lax.rem(parity + turn, 2) * 32
        for row, col, place, shift_parity in chips:
            if shift_parity == turn:
                copy(source.at[first + place], target.at[me], k, row + half, col)

    def finish_copies(source, target, k):
        part = pl.ds(0, 127)
        await_bytes(source.at[part], sent.at[k])
        await_bytes(target.at[part], got.at[k])

    pack(send_t, 0, 64)
    pl.semaphore_wait(entered, 15)
    chip_place = (r // 2) * 8 + c
    recv_t[chip_place] = send_t[chip_place]
    for row, col, _, _ in chips:
        copy(send_t.at[row * 4 + col], recv_t.at[chip_place], 12, row + core, col)

    for k in range(7, 11):
        loads[k].wait()
    for t, source in enumerate((out_w_ref, in_w_ref)):
        for w in range(4):
            turned = _flip(source[w])
            for quarter in range(4):
                place = t * 768 + quarter * 128 + w * 32
                weights[place : place + 32] = turned[quarter * 32 : quarter * 32 + 32]
        for w in (4, 5):
            weights[t * 768 + w * 128 : t * 768 + w * 128 + 128] = _flip(source[w])
    for w in range(2):
        tin_t[w * 512 : w * 512 + 512] = _flip(tin_ref[w])
    tout_t[...] = _flip(tout_ref[...])
    loads[0].wait()
    for a in range(16):
        natural = jnp.concatenate([pair_ref[a], pair_ref[a + 16]], 0).astype(jnp.float32)
        state[:, a * 128 : a * 128 + 128] = jnp.transpose(natural)
        row = lax.broadcasted_iota(jnp.int32, (128, 128), 0)
        lane = lax.broadcasted_iota(jnp.int32, (128, 128), 1)
        right_token = jnp.where(row % 8 >= 4, row // 8 * 4 + row % 8 - 4, -1)
        spreader[:128, a * 128 : a * 128 + 128] = _ones_where(lane % 64 == right_token)
        left_token = jnp.where(row % 16 < 4, row // 16 * 4 + row % 16, -1)
        spreader[128:, a * 128 : a * 128 + 128] = _ones_where(
            jnp.where(lane < 64, a, a + 16) == left_token
        )
    loads[6].wait()
    await_bytes(send_t.at[pl.ds(0, 63)], sent.at[12])
    await_bytes(recv_t.at[pl.ds(0, 63)], got.at[12])

    total = jnp.zeros((16, 128), jnp.float32)
    for d in range(0, 64, 32):
        total = total + jnp.sum(recv_t[d : d + 32].astype(jnp.float32), 0)
    count = jnp.maximum(total[12:], 1.0)
    single = jnp.concatenate([total[4 * m : 4 * m + 4] / count for m in range(3)], 1)
    proj = _dot(single.astype(jnp.bfloat16), token_out_ref[...])
    share[...] = jnp.zeros_like(share)
    for m in range(3):
        share[4 * m : 4 * m + 4] = proj[:, m * 128 : (m + 1) * 128]

    recv_row[c] = share[...]
    column = me // 16
    place = lax.rem(me, 16)
    for step in range(1, 16):
        row = lax.rem(r + step, 16)
        copy(share.at[pl.ds(0, 8)], recv_right.at[place], 10, row, column)

    @pl.when(column == c)
    def _():
        recv_right[place] = share[pl.ds(0, 8)]

    @pl.when(column != c)
    def _():
        copy(share.at[pl.ds(0, 8)], recv_right.at[place], 10, r, column)

    for step in range(1, 8):
        copy(share, recv_row.at[c], 13, r, lax.rem(c + step, 8))

    @pl.when(column != c)
    def _():
        await_bytes(recv_right.at[pl.ds(0, 1)], sent.at[10])

    await_bytes(recv_right.at[pl.ds(0, 15)], sent.at[10])
    await_bytes(recv_row.at[pl.ds(0, 7)], sent.at[13])

    mine = (me >= 16 * c) & (me < 16 * c + 16)

    @pl.when(mine)
    def _():
        await_bytes(recv_right.at[pl.ds(0, 15)], got.at[10])

    @pl.when(jnp.logical_not(mine))
    def _():
        await_bytes(recv_right, got.at[10])

    await_bytes(recv_row.at[pl.ds(0, 7)], got.at[13])
    def spans(width, step):
        if width == 2048:
            step(0)
        else:
            lax.fori_loop(0, 2048 // width, lambda g, _: (step(g), 0)[1], 0)

    def lanes(g, width):
        return pl.ds(g * width if isinstance(g, int) else pl.multiple_of(g * width, width), width)

    over_rows = (((0,), (0,)), ((), ()))
    rows = jnp.concatenate(
        [recv_right[...].reshape(128, 128), recv_row[...].reshape(128, 128)], 0
    )
    high = rows.astype(jnp.bfloat16)
    low = (rows - high.astype(jnp.float32)).astype(jnp.bfloat16)

    def start_state(g):
        here = lanes(g, START)
        spread = spreader[:, here]
        started = (
            state[:, here]
            + lax.dot_general(high, spread, over_rows, preferred_element_type=jnp.float32)
            + lax.dot_general(low, spread, over_rows, preferred_element_type=jnp.float32)
        )
        state[:, here] = started
        normed[:, here] = _norm(started).astype(jnp.bfloat16)

    spans(START, start_state)

    def edges(t, half, turn, target):
        quarter = half * 2 + lax.rem(parity + turn, 2)
        stage = (half * 2 + turn) * 1024
        place = pl.ds(pl.multiple_of(t * 768 + quarter * 128, 128), 128)

        def chunk(g):
            both = _dot(weights[place, :], normed[:, lanes(g, EDGE)])
            left = _sigmoid(both[:32]) * both[32:64]
            right = _sigmoid(both[64:96]) * both[96:]
            for h in range(EDGE // 128):
                a = stage + g * (EDGE // 128) + h
                part = slice(h * 128, h * 128 + 128)
                edge32[pl.ds(a, 32, stride=32), :] = left[:, part]
                edge32[pl.ds(a + 16, 32, stride=32), :] = right[:, part]

        spans(EDGE, chunk)
        target[pl.ds(quarter * 32, 32)] = (
            edge32[stage : stage + 1024].reshape(32, 32, 128).astype(jnp.bfloat16)
        )

    def gates(base):
        def chunk(g):
            gate[:, lanes(g, EDGE)] = _sigmoid(
                _dot(weights[pl.ds((base + 4) * 128, 128), :], normed[:, lanes(g, EDGE)])
            )

        spans(EDGE, chunk)

    low_lanes = lax.broadcasted_iota(jnp.int32, (16, 128), 1) < 64

    def assemble(source, first, target):
        def block(g, _):
            for k in range(ROWS):
                row = g * ROWS + k
                for q in range(4):
                    even = source[row * 8 + 2 * q, first : first + 16]
                    odd = source[row * 8 + 2 * q + 1, first : first + 16]
                    target[pl.ds(row * 32, 16), pl.ds(q * 128, 128)] = jnp.where(
                        low_lanes, even, pltpu.roll(odd, 64, 1)
                    )
                    target[pl.ds(row * 32 + 16, 16), pl.ds(q * 128, 128)] = jnp.where(
                        low_lanes, pltpu.roll(even, 64, 1), odd
                    )
            return 0

        lax.fori_loop(0, 16 // ROWS, block, 0)

    def split(source, target):
        def block(g, _):
            for k in range(ROWS):
                row = g * ROWS + k
                for q in range(4):
                    top = source[pl.ds(row * 32, 16), pl.ds(q * 128, 128)]
                    low = source[pl.ds(row * 32 + 16, 16), pl.ds(q * 128, 128)]
                    target[row * 8 + 2 * q] = jnp.where(low_lanes, top, pltpu.roll(low, 64, 1))
                    target[row * 8 + 2 * q + 1] = jnp.where(low_lanes, pltpu.roll(top, 64, 1), low)
            return 0

        lax.fori_loop(0, 16 // ROWS, block, 0)

    def triangle(t, width, beside, after):
        base = 6 * t
        for half in range(2):
            for turn in range(2):
                edges(t, half, turn, send_e.at[t])
                launch_quarter(send_e.at[t], recv_e.at[t], 2 * t, half, turn)
        copy(send_e.at[t, sibling_channel], recv_e.at[t, me], 2 * t, sibling, c)
        recv_e[t, me] = send_e[t, channel]
        gates(base)
        finish_copies(send_e.at[t], recv_e.at[t], 2 * t)
        assemble(recv_e.at[t], 0, mat_l)
        assemble(recv_e.at[t], 16, mat_r)
        axis = 1 - t
        mat_p[...] = lax.dot_general(
            mat_l[...],
            mat_r[...],
            (((axis,), (axis,)), ((), ())),
            preferred_element_type=jnp.float32,
        ).astype(jnp.bfloat16)
        split(mat_p, send_p.at[t])
        launch(send_p.at[t], recv_p.at[t], 2 * t + 1, channel)
        beside()
        finish_copies(send_p.at[t], recv_p.at[t], 2 * t + 1)

        if t == 0:
            for step in range(1, 16):
                copy(add32, recv_add.at[r], 11, lax.rem(r + step, 16), c)
        rows32[...] = recv_p[t].astype(jnp.float32).reshape(2048, 128)

        def close(g):
            count = width // 128
            product = jnp.concatenate(
                [rows32[pl.ds(g * count + h, 128, stride=16), :] for h in range(count)], 1
            )
            product = _norm(product).astype(jnp.bfloat16)
            here = lanes(g, width)
            updated = state[:, here] + gate[:, here] * _dot(
                weights[pl.ds((base + 5) * 128, 128), :], product
            )
            after(g, width, updated)

        spans(width, close)

    def next_update(g, width, updated):
        state[:, lanes(g, width)] = updated
        normed[:, lanes(g, width)] = _norm(updated).astype(jnp.bfloat16)

    def transition(g, width, updated):
        inner = _dot(tin_t[...], _norm(updated).astype(jnp.bfloat16))
        up = inner[:512]
        hidden = (up * _sigmoid(up) * inner[512:]).astype(jnp.bfloat16)
        final = updated + _dot(tout_t[...], hidden)
        for h in range(width // 128):
            natural = jnp.transpose(final[:, h * 128 : (h + 1) * 128]).astype(jnp.bfloat16)
            result_ref[g * (width // 128) + h] = natural[:64]
            result_ref[g * (width // 128) + h + 16] = natural[64:]

    def share_added():
        for j in range(8):
            add32[4 * j : 4 * j + 4] = recv_row[j, 8:12]
        recv_add[r] = add32[...]

    def finish_atoms():
        await_bytes(recv_add.at[pl.ds(0, 15)], sent.at[11])
        await_bytes(recv_add.at[pl.ds(0, 15)], got.at[11])
        added = recv_add[...].reshape(512, 128)
        high = added.astype(jnp.bfloat16)
        low = (added - high.astype(jnp.float32)).astype(jnp.bfloat16)
        token = lax.broadcasted_iota(jnp.int32, (512, 128), 0)
        chosen = _ones_where(token == any_token[:1])
        picked = lax.dot_general(
            chosen, high, over_rows, preferred_element_type=jnp.float32
        ) + lax.dot_general(chosen, low, over_rows, preferred_element_type=jnp.float32)
        atoms_out_ref[...] = (mid[...] + picked[:SLOTS]).astype(jnp.bfloat16)

    triangle(0, CLOSE, share_added, next_update)
    triangle(1, LAST, finish_atoms, transition)


def body(pair_in, atoms_in, atom_token, atom_mask, *parameters):
    vmem = pl.BlockSpec(memory_space=pltpu.VMEM)
    staged = (pair_in, atoms_in, *parameters)
    bf16, f32 = jnp.bfloat16, jnp.float32
    return pl.pallas_call(
        _kernel,
        out_shape=(
            jax.ShapeDtypeStruct(pair_in.shape, bf16),
            jax.ShapeDtypeStruct(atoms_in.shape, bf16),
        ),
        in_specs=[vmem] * 2 + [pl.BlockSpec(memory_space=pltpu.HBM)] * 11,
        out_specs=(vmem, vmem),
        scratch_shapes=[pltpu.VMEM(array.shape, array.dtype) for array in staged]
        + [
            pltpu.VMEM((128, 2048), f32),
            pltpu.VMEM((128, 2048), bf16),
            pltpu.VMEM((128, 2048), f32),
            pltpu.VMEM((2048, 128), f32),
            pltpu.VMEM((1536, 128), bf16),
            pltpu.VMEM((1024, 128), bf16),
            pltpu.VMEM((128, 512), bf16),
        ]
        + [pltpu.VMEM((2, 128, 32, 128), bf16)] * 2
        + [pltpu.VMEM((4096, 128), f32)]
        + [pltpu.VMEM((2, 128, 16, 128), bf16)] * 2
        + [pltpu.VMEM((512, 512), bf16)] * 3
        + [
            pltpu.VMEM((2, 64, 128), bf16),
            pltpu.VMEM((2, 64, 128), bf16),
            pltpu.VMEM((16, 128), f32),
            pltpu.VMEM((2, 8, 128), jnp.int32),
            pltpu.VMEM((8, 128), jnp.int32),
            pltpu.VMEM((WIDE, 128), bf16),
            pltpu.VMEM((SLOTS, 128), f32),
            pltpu.VMEM((2, 128, 512), bf16),
            pltpu.VMEM((64, 16, 128), bf16),
            pltpu.VMEM((64, 16, 128), bf16),
            pltpu.VMEM((16, 128), f32),
            pltpu.VMEM((8, 16, 128), f32),
            pltpu.VMEM((16, 8, 128), f32),
            pltpu.VMEM((256, 2048), bf16),
            pltpu.VMEM((32, 128), f32),
            pltpu.VMEM((16, 32, 128), f32),
            pltpu.SemaphoreType.DMA((14,)),
            pltpu.SemaphoreType.DMA((14,)),
            pltpu.SemaphoreType.REGULAR,
            pltpu.SemaphoreType.DMA((11,)),
        ],
        compiler_params=pltpu.CompilerParams(
            collective_id=0, has_side_effects=True, vmem_limit_bytes=60 * 1024 * 1024
        ),
        name="atoms_and_pair",
    )(atom_token.reshape(1, SLOTS), atom_mask.reshape(1, SLOTS), *staged)


def solution(mesh):
    placed = (
        P("row", "col", None),
        P(("row", "col"), None),
        P(("row", "col")),
        P(("row", "col")),
        P(),
        P(),
        P(),
        P(),
        P(),
        P(),
        P(),
        P(),
        P(),
    )
    return jax.shard_map(
        body,
        mesh=mesh,
        in_specs=placed,
        out_specs=(P("row", "col", None), P(("row", "col"), None)),
        check_vma=False,
    )
```

```python
import jax
import jax.numpy as jnp
from jax import lax
from jax.experimental import pallas as pl
from jax.experimental.pallas import tpu as pltpu
from jax.sharding import PartitionSpec as P

HEADS = 4
QWIN = 32
KWIN = 128
SIDE = 48
SLOTS = 96
WIDE = SLOTS + 2 * SIDE
START = 2048
EDGE = 2048
CLOSE = 2048
LAST = 1024
ROWS = 16

epsilon = 1e-05

def _far_first():
    shifts = [(x, y, z) for x in range(4) for y in range(4) for z in range(4)][1:]
    return sorted(shifts, key=lambda shift: -sum(min(s, 4 - s) for s in shift))


def _chips(r, c):
    z, y, x = r // 4, lax.rem(c, 2) * 2 + lax.rem(r // 2, 2), c // 2
    xs, ys, zs = [[lax.rem(v + s, 4) for s in range(4)] for v in (x, y, z)]
    row_y = [lax.rem(v, 2) * 2 for v in ys]
    col_y = [v // 2 for v in ys]

    def chip(dx, dy, dz):
        row = zs[dz] * 4 + row_y[dy]
        return row, xs[dx] * 2 + col_y[dy], xs[dx] * 8 + ys[dy] * 2 + zs[dz] // 2

    others = [chip(*shift) + (sum(shift) % 2,) for shift in _far_first()]
    return chip(0, 0, 0)[2], lax.rem(x + y + z, 2), others


def _sigmoid(x):
    return 0.5 * jnp.tanh(0.5 * x) + 0.5


def _norm(x):
    center = x - jnp.mean(x, 0, keepdims=True)
    spread = jnp.mean(center * center, 0, keepdims=True)
    return center * lax.rsqrt(spread + epsilon)


def _dot(a, b):
    return jnp.dot(a, b, preferred_element_type=jnp.float32)


def _flip(x):
    return jnp.transpose(x.astype(jnp.float32)).astype(jnp.bfloat16)


def _norm_rows(x):
    center = x - jnp.mean(x, -1, keepdims=True)
    spread = jnp.mean(center * center, -1, keepdims=True)
    return center * lax.rsqrt(spread + epsilon)


def _ones_where(condition):
    return jnp.where(condition, 1.0, 0.0).astype(jnp.bfloat16)


def _kernel(
    token_ref, mask_ref, *refs,
):
    sources, refs = refs[:11], refs[11:]
    result_ref, atoms_out_ref, *refs = refs
    staged, refs = refs[:11], refs[11:]
    (pair_ref, atoms_ref, atom_w_ref, atom_tin_ref, atom_tout_ref,
     token_in_ref, token_out_ref, out_w_ref, in_w_ref, tin_ref, tout_ref) = staged
    (    state, normed, gate, rows32, weights, tin_t, tout_t,
    send_e, recv_e, edge32, send_p, recv_p, mat_l, mat_r, mat_p,
    halo_out, halo_in, flags, live_token, any_token, wide, mid, featured,
    send_t, recv_t, share, recv_row, recv_right, spreader, add32, recv_add,
    sent, got, entered, loaded) = refs
    r = lax.axis_index("row")
    c = lax.axis_index("col")
    me = r * 8 + c
    spot, parity, chips = _chips(r, c)
    core = lax.rem(r, 2)
    sibling = r + 1 - 2 * core
    channel = core * 64 + parity * 32 + spot
    sibling_channel = (1 - core) * 64 + parity * 32 + spot
    barrier = pltpu.get_barrier_semaphore()
    after = lax.rem(me + 1, 128)
    before = lax.rem(me + 127, 128)

    def greet(semaphore, row, col):
        pl.semaphore_signal(
            semaphore, inc=1, device_id=(row, col), device_id_type=pl.DeviceIdType.MESH
        )

    def copy(source, target, k, row, col):
        pltpu.make_async_remote_copy(
            src_ref=source,
            dst_ref=target,
            send_sem=sent.at[k],
            recv_sem=got.at[k],
            device_id=(row, col),
            device_id_type=pl.DeviceIdType.MESH,
        ).start()

    def await_bytes(ref, semaphore):
        pltpu.make_async_copy(ref, ref, semaphore).wait()

    greet(barrier, after // 8, lax.rem(after, 8))
    greet(barrier, before // 8, lax.rem(before, 8))
    for step in range(1, 8):
        greet(barrier, r, lax.rem(c + step, 8))
    for step in range(1, 16):
        greet(barrier, lax.rem(r + step, 16), c)

    loads = [
        pltpu.make_async_copy(source, place, loaded.at[k])
        for k, (source, place) in enumerate(zip(sources, staged))
    ]
    for k in (1, 2, 3, 4, 5, 6, 0, 7, 8, 9, 10):
        loads[k].start()

    flags[...] = jnp.zeros_like(flags)
    flags[:, :SLOTS] = jnp.broadcast_to(
        jnp.where(mask_ref[...] == 1, 1.0, 0.0), (16, SLOTS)
    )
    featured[0] = jnp.zeros((128, 512), jnp.bfloat16)
    featured[0, :SLOTS, 384:] = jnp.ones((SLOTS, 128), jnp.bfloat16)
    any_token[...] = jnp.full_like(any_token, -1)
    any_token[:, :SLOTS] = jnp.broadcast_to(token_ref[...], (8, SLOTS))
    own_flags = flags[...].astype(jnp.bfloat16)
    loads[1].wait()
    halo_out[0, :SIDE] = atoms_ref[SLOTS - SIDE :]
    halo_out[1, :SIDE] = atoms_ref[:SIDE]
    halo_out[0, SIDE:] = own_flags
    halo_out[1, SIDE:] = own_flags
    live_token[0] = jnp.where(flags[:8] > 0.5, any_token[...], -1)
    pl.semaphore_wait(barrier, 24)
    copy(halo_out.at[0], halo_in.at[0], 6, after // 8, lax.rem(after, 8))
    copy(halo_out.at[1], halo_in.at[1], 7, before // 8, lax.rem(before, 8))
    for step in range(1, 16):
        greet(entered, lax.rem(r + step, 16), c)

    own = atoms_ref[...].astype(jnp.float32)
    own_normed = _norm_rows(own).astype(jnp.bfloat16)
    wide[SIDE : SIDE + SLOTS] = own_normed
    loads[2].wait()
    queries = _dot(own_normed, atom_w_ref[0]).astype(jnp.bfloat16)
    atom_gate = _sigmoid(_dot(own_normed, atom_w_ref[3]))
    for k in (6, 7):
        await_bytes(halo_out.at[k - 6], sent.at[k])
        await_bytes(halo_in.at[k - 6], got.at[k])
    wide[:SIDE] = _norm_rows(halo_in[0, :SIDE].astype(jnp.float32)).astype(jnp.bfloat16)
    wide[SIDE + SLOTS :] = _norm_rows(halo_in[1, :SIDE].astype(jnp.float32)).astype(jnp.bfloat16)
    keys = _dot(wide[...], atom_w_ref[1]).astype(jnp.bfloat16)
    values = _dot(wide[...], atom_w_ref[2]).astype(jnp.bfloat16)
    slot = lax.broadcasted_iota(jnp.int32, (128, WIDE), 0)
    key = lax.broadcasted_iota(jnp.int32, (128, WIDE), 1)
    keep = (
        _dot(halo_in[0, SIDE:], _ones_where((key + SIDE == slot) & (me > 0)))
        + _dot(own_flags, _ones_where(key - SIDE == slot))
        + _dot(halo_in[1, SIDE:], _ones_where((key - SIDE - SLOTS == slot) & (me < 127)))
    )[:1]
    query = lax.broadcasted_iota(jnp.int32, (SLOTS, WIDE), 0)
    key = lax.broadcasted_iota(jnp.int32, (SLOTS, WIDE), 1)
    offset = key - (query // QWIN) * QWIN
    inside = (offset >= 0) & (offset < KWIN)
    allowed = jnp.where(inside & ((keep > 0.5) | (key - SIDE == query)), 1.0, 0.0)
    lane_head = lax.broadcasted_iota(jnp.int32, (SLOTS, 128), 1) // 32
    stacked = jnp.concatenate(
        [jnp.where(lane_head == h, queries.astype(jnp.float32), 0.0) for h in range(HEADS)], 0
    ).astype(jnp.bfloat16)
    scores = (
        lax.dot_general(
            stacked, keys, (((1,), (1,)), ((), ())), preferred_element_type=jnp.float32
        )
        * 32**-0.5
    )
    raw = jnp.where(jnp.concatenate([allowed] * HEADS, 0) > 0.5, jnp.exp(scores), 0.0)
    attention = (raw / jnp.sum(raw, -1, keepdims=True)).astype(jnp.bfloat16)
    spread = _dot(attention, values)
    attended = jnp.zeros((SLOTS, 128), jnp.float32)
    for h in range(HEADS):
        attended = attended + jnp.where(lane_head == h, spread[h * SLOTS : (h + 1) * SLOTS], 0.0)
    gated = (atom_gate * attended).astype(jnp.bfloat16)
    resid = own + _dot(gated, atom_w_ref[4])
    resid_normed = _norm_rows(resid).astype(jnp.bfloat16)
    for k in (3, 4, 5):
        loads[k].wait()
    up = _dot(resid_normed, atom_tin_ref[0])
    hidden = (up * _sigmoid(up) * _dot(resid_normed, atom_tin_ref[1])).astype(jnp.bfloat16)
    atom_mid = resid + _dot(hidden, atom_tout_ref[...])
    mid[...] = atom_mid
    feature = jnp.maximum(_dot(atom_mid.astype(jnp.bfloat16), token_in_ref[...]), 0.0)
    featured[0, :SLOTS, :384] = feature.astype(jnp.bfloat16)
    copy(featured.at[0], featured.at[1], 8, sibling, c)
    copy(live_token.at[0], live_token.at[1], 9, sibling, c)

    await_bytes(featured.at[0], sent.at[8])
    await_bytes(live_token.at[0], sent.at[9])
    await_bytes(featured.at[1], got.at[8])
    await_bytes(live_token.at[1], got.at[9])
    slots_token = jnp.concatenate([live_token[0, :1], live_token[1, :1]], 1)
    both = featured[...].reshape(256, 512)
    place = lax.broadcasted_iota(jnp.int32, (64, 256), 0)
    owner = place // 8 * 16 + core * 8 + place % 8
    for t in range(4):
        sums = _dot(_ones_where(owner * 4 + t == slots_token), both)
        for m in range(4):
            rows32[pl.ds(4 * m + t, 64, stride=16), :] = sums[:, m * 128 : (m + 1) * 128]

    def pack(target, first, count):
        target[first : first + count] = (
            rows32[first * 16 : (first + count) * 16].reshape(count, 16, 128).astype(jnp.bfloat16)
        )

    def launch(source, target, k, slot):
        target[slot] = source[me]
        for half in range(2):
            for row, col, _, _ in chips:
                copy(source.at[row * 8 + half * 8 + col], target.at[slot], k, row + half, col)
        copy(source.at[sibling * 8 + c], target.at[slot], k, sibling, c)

    def launch_quarter(source, target, k, half, turn):
        first = half * 64 + lax.rem(parity + turn, 2) * 32
        for row, col, place, shift_parity in chips:
            if shift_parity == turn:
                copy(source.at[first + place], target.at[me], k, row + half, col)

    def finish_copies(source, target, k):
        part = pl.ds(0, 127)
        await_bytes(source.at[part], sent.at[k])
        await_bytes(target.at[part], got.at[k])

    pack(send_t, 0, 64)
    pl.semaphore_wait(entered, 15)
    chip_place = (r // 2) * 8 + c
    recv_t[chip_place] = send_t[chip_place]
    for row, col, _, _ in chips:
        copy(send_t.at[row * 4 + col], recv_t.at[chip_place], 12, row + core, col)

    for k in range(7, 11):
        loads[k].wait()
    for t, source in enumerate((out_w_ref, in_w_ref)):
        for w in range(4):
            turned = _flip(source[w])
            for quarter in range(4):
                place = t * 768 + quarter * 128 + w * 32
                weights[place : place + 32] = turned[quarter * 32 : quarter * 32 + 32]
        for w in (4, 5):
            weights[t * 768 + w * 128 : t * 768 + w * 128 + 128] = _flip(source[w])
    for w in range(2):
        tin_t[w * 512 : w * 512 + 512] = _flip(tin_ref[w])
    tout_t[...] = _flip(tout_ref[...])
    loads[0].wait()
    for a in range(16):
        natural = jnp.concatenate([pair_ref[a], pair_ref[a + 16]], 0).astype(jnp.float32)
        state[:, a * 128 : a * 128 + 128] = jnp.transpose(natural)
        row = lax.broadcasted_iota(jnp.int32, (128, 128), 0)
        lane = lax.broadcasted_iota(jnp.int32, (128, 128), 1)
        right_token = jnp.where(row % 8 >= 4, row // 8 * 4 + row % 8 - 4, -1)
        spreader[:128, a * 128 : a * 128 + 128] = _ones_where(lane % 64 == right_token)
        left_token = jnp.where(row % 16 < 4, row // 16 * 4 + row % 16, -1)
        spreader[128:, a * 128 : a * 128 + 128] = _ones_where(
            jnp.where(lane < 64, a, a + 16) == left_token
        )
    loads[6].wait()
    await_bytes(send_t.at[pl.ds(0, 63)], sent.at[12])
    await_bytes(recv_t.at[pl.ds(0, 63)], got.at[12])

    total = jnp.zeros((16, 128), jnp.float32)
    for d in range(0, 64, 32):
        total = total + jnp.sum(recv_t[d : d + 32].astype(jnp.float32), 0)
    count = jnp.maximum(total[12:], 1.0)
    single = jnp.concatenate([total[4 * m : 4 * m + 4] / count for m in range(3)], 1)
    proj = _dot(single.astype(jnp.bfloat16), token_out_ref[...])
    share[...] = jnp.zeros_like(share)
    for m in range(3):
        share[4 * m : 4 * m + 4] = proj[:, m * 128 : (m + 1) * 128]

    recv_row[c] = share[...]
    column = me // 16
    place = lax.rem(me, 16)
    for step in range(1, 16):
        row = lax.rem(r + step, 16)
        copy(share.at[pl.ds(0, 8)], recv_right.at[place], 10, row, column)

    @pl.when(column == c)
    def _():
        recv_right[place] = share[pl.ds(0, 8)]

    @pl.when(column != c)
    def _():
        copy(share.at[pl.ds(0, 8)], recv_right.at[place], 10, r, column)

    for step in range(1, 8):
        copy(share, recv_row.at[c], 13, r, lax.rem(c + step, 8))

    @pl.when(column != c)
    def _():
        await_bytes(recv_right.at[pl.ds(0, 1)], sent.at[10])

    await_bytes(recv_right.at[pl.ds(0, 15)], sent.at[10])
    await_bytes(recv_row.at[pl.ds(0, 7)], sent.at[13])

    mine = (me >= 16 * c) & (me < 16 * c + 16)

    @pl.when(mine)
    def _():
        await_bytes(recv_right.at[pl.ds(0, 15)], got.at[10])

    @pl.when(jnp.logical_not(mine))
    def _():
        await_bytes(recv_right, got.at[10])

    await_bytes(recv_row.at[pl.ds(0, 7)], got.at[13])
    def spans(width, step):
        if width == 2048:
            step(0)
        else:
            lax.fori_loop(0, 2048 // width, lambda g, _: (step(g), 0)[1], 0)

    def lanes(g, width):
        return pl.ds(g * width if isinstance(g, int) else pl.multiple_of(g * width, width), width)

    over_rows = (((0,), (0,)), ((), ()))
    rows = jnp.concatenate(
        [recv_right[...].reshape(128, 128), recv_row[...].reshape(128, 128)], 0
    )
    high = rows.astype(jnp.bfloat16)
    low = (rows - high.astype(jnp.float32)).astype(jnp.bfloat16)

    def start_state(g):
        here = lanes(g, START)
        spread = spreader[:, here]
        started = (
            state[:, here]
            + lax.dot_general(high, spread, over_rows, preferred_element_type=jnp.float32)
            + lax.dot_general(low, spread, over_rows, preferred_element_type=jnp.float32)
        )
        state[:, here] = started
        normed[:, here] = _norm(started).astype(jnp.bfloat16)

    spans(START, start_state)

    def edges(t, half, turn, target):
        quarter = half * 2 + lax.rem(parity + turn, 2)
        stage = (half * 2 + turn) * 1024
        place = pl.ds(pl.multiple_of(t * 768 + quarter * 128, 128), 128)

        def chunk(g):
            both = _dot(weights[place, :], normed[:, lanes(g, EDGE)])
            left = _sigmoid(both[:32]) * both[32:64]
            right = _sigmoid(both[64:96]) * both[96:]
            for h in range(EDGE // 128):
                a = stage + g * (EDGE // 128) + h
                part = slice(h * 128, h * 128 + 128)
                edge32[pl.ds(a, 32, stride=32), :] = left[:, part]
                edge32[pl.ds(a + 16, 32, stride=32), :] = right[:, part]

        spans(EDGE, chunk)
        target[pl.ds(quarter * 32, 32)] = (
            edge32[stage : stage + 1024].reshape(32, 32, 128).astype(jnp.bfloat16)
        )

    def gates(base):
        def chunk(g):
            gate[:, lanes(g, EDGE)] = _sigmoid(
                _dot(weights[pl.ds((base + 4) * 128, 128), :], normed[:, lanes(g, EDGE)])
            )

        spans(EDGE, chunk)

    low_lanes = lax.broadcasted_iota(jnp.int32, (16, 128), 1) < 64

    def assemble(source, first, target):
        def block(g, _):
            for k in range(ROWS):
                row = g * ROWS + k
                for q in range(4):
                    even = source[row * 8 + 2 * q, first : first + 16]
                    odd = source[row * 8 + 2 * q + 1, first : first + 16]
                    target[pl.ds(row * 32, 16), pl.ds(q * 128, 128)] = jnp.where(
                        low_lanes, even, pltpu.roll(odd, 64, 1)
                    )
                    target[pl.ds(row * 32 + 16, 16), pl.ds(q * 128, 128)] = jnp.where(
                        low_lanes, pltpu.roll(even, 64, 1), odd
                    )
            return 0

        lax.fori_loop(0, 16 // ROWS, block, 0)

    def split(source, target):
        def block(g, _):
            for k in range(ROWS):
                row = g * ROWS + k
                for q in range(4):
                    top = source[pl.ds(row * 32, 16), pl.ds(q * 128, 128)]
                    low = source[pl.ds(row * 32 + 16, 16), pl.ds(q * 128, 128)]
                    target[row * 8 + 2 * q] = jnp.where(low_lanes, top, pltpu.roll(low, 64, 1))
                    target[row * 8 + 2 * q + 1] = jnp.where(low_lanes, pltpu.roll(top, 64, 1), low)
            return 0

        lax.fori_loop(0, 16 // ROWS, block, 0)

    def triangle(t, width, beside, after):
        base = 6 * t
        for half in range(2):
            for turn in range(2):
                edges(t, half, turn, send_e.at[t])
                launch_quarter(send_e.at[t], recv_e.at[t], 2 * t, half, turn)
        copy(send_e.at[t, sibling_channel], recv_e.at[t, me], 2 * t, sibling, c)
        recv_e[t, me] = send_e[t, channel]
        gates(base)
        finish_copies(send_e.at[t], recv_e.at[t], 2 * t)
        assemble(recv_e.at[t], 0, mat_l)
        assemble(recv_e.at[t], 16, mat_r)
        axis = 1 - t
        mat_p[...] = lax.dot_general(
            mat_l[...],
            mat_r[...],
            (((axis,), (axis,)), ((), ())),
            preferred_element_type=jnp.float32,
        ).astype(jnp.bfloat16)
        split(mat_p, send_p.at[t])
        launch(send_p.at[t], recv_p.at[t], 2 * t + 1, channel)
        beside()
        finish_copies(send_p.at[t], recv_p.at[t], 2 * t + 1)

        if t == 0:
            for step in range(1, 16):
                copy(add32, recv_add.at[r], 11, lax.rem(r + step, 16), c)
        rows32[...] = recv_p[t].astype(jnp.float32).reshape(2048, 128)

        def close(g):
            count = width // 128
            product = jnp.concatenate(
                [rows32[pl.ds(g * count + h, 128, stride=16), :] for h in range(count)], 1
            )
            product = _norm(product).astype(jnp.bfloat16)
            here = lanes(g, width)
            updated = state[:, here] + gate[:, here] * _dot(
                weights[pl.ds((base + 5) * 128, 128), :], product
            )
            after(g, width, updated)

        spans(width, close)

    def next_update(g, width, updated):
        state[:, lanes(g, width)] = updated
        normed[:, lanes(g, width)] = _norm(updated).astype(jnp.bfloat16)

    def transition(g, width, updated):
        inner = _dot(tin_t[...], _norm(updated).astype(jnp.bfloat16))
        up = inner[:512]
        hidden = (up * _sigmoid(up) * inner[512:]).astype(jnp.bfloat16)
        final = updated + _dot(tout_t[...], hidden)
        for h in range(width // 128):
            natural = jnp.transpose(final[:, h * 128 : (h + 1) * 128]).astype(jnp.bfloat16)
            result_ref[g * (width // 128) + h] = natural[:64]
            result_ref[g * (width // 128) + h + 16] = natural[64:]

    def share_added():
        for j in range(8):
            add32[4 * j : 4 * j + 4] = recv_row[j, 8:12]
        recv_add[r] = add32[...]

    def finish_atoms():
        await_bytes(recv_add.at[pl.ds(0, 15)], sent.at[11])
        await_bytes(recv_add.at[pl.ds(0, 15)], got.at[11])
        added = recv_add[...].reshape(512, 128)
        high = added.astype(jnp.bfloat16)
        low = (added - high.astype(jnp.float32)).astype(jnp.bfloat16)
        token = lax.broadcasted_iota(jnp.int32, (512, 128), 0)
        chosen = _ones_where(token == any_token[:1])
        picked = lax.dot_general(
            chosen, high, over_rows, preferred_element_type=jnp.float32
        ) + lax.dot_general(chosen, low, over_rows, preferred_element_type=jnp.float32)
        atoms_out_ref[...] = (mid[...] + picked[:SLOTS]).astype(jnp.bfloat16)

    triangle(0, CLOSE, share_added, next_update)
    triangle(1, LAST, finish_atoms, transition)


def body(pair_in, atoms_in, atom_token, atom_mask, *parameters):
    vmem = pl.BlockSpec(memory_space=pltpu.VMEM)
    staged = (pair_in, atoms_in, *parameters)
    bf16, f32 = jnp.bfloat16, jnp.float32
    pair_out, atoms_out = pl.pallas_call(
        _kernel,
        out_shape=(
            jax.ShapeDtypeStruct(pair_in.shape, bf16),
            jax.ShapeDtypeStruct(atoms_in.shape, bf16),
        ),
        in_specs=[vmem] * 2 + [pl.BlockSpec(memory_space=pltpu.HBM)] * 11,
        out_specs=(vmem, vmem),
        scratch_shapes=[pltpu.VMEM(array.shape, array.dtype) for array in staged]
        + [
            pltpu.VMEM((128, 2048), f32),
            pltpu.VMEM((128, 2048), bf16),
            pltpu.VMEM((128, 2048), f32),
            pltpu.VMEM((2048, 128), f32),
            pltpu.VMEM((1536, 128), bf16),
            pltpu.VMEM((1024, 128), bf16),
            pltpu.VMEM((128, 512), bf16),
        ]
        + [pltpu.VMEM((2, 128, 32, 128), bf16)] * 2
        + [pltpu.VMEM((4096, 128), f32)]
        + [pltpu.VMEM((2, 128, 16, 128), bf16)] * 2
        + [pltpu.VMEM((512, 512), bf16)] * 3
        + [
            pltpu.VMEM((2, 64, 128), bf16),
            pltpu.VMEM((2, 64, 128), bf16),
            pltpu.VMEM((16, 128), f32),
            pltpu.VMEM((2, 8, 128), jnp.int32),
            pltpu.VMEM((8, 128), jnp.int32),
            pltpu.VMEM((WIDE, 128), bf16),
            pltpu.VMEM((SLOTS, 128), f32),
            pltpu.VMEM((2, 128, 512), bf16),
            pltpu.VMEM((64, 16, 128), bf16),
            pltpu.VMEM((64, 16, 128), bf16),
            pltpu.VMEM((16, 128), f32),
            pltpu.VMEM((8, 16, 128), f32),
            pltpu.VMEM((16, 8, 128), f32),
            pltpu.VMEM((256, 2048), bf16),
            pltpu.VMEM((32, 128), f32),
            pltpu.VMEM((16, 32, 128), f32),
            pltpu.SemaphoreType.DMA((14,)),
            pltpu.SemaphoreType.DMA((14,)),
            pltpu.SemaphoreType.REGULAR,
            pltpu.SemaphoreType.DMA((11,)),
        ],
        compiler_params=pltpu.CompilerParams(
            collective_id=0, has_side_effects=True, vmem_limit_bytes=60 * 1024 * 1024
        ),
        name="atoms_and_pair",
    )(atom_token.reshape(1, SLOTS), atom_mask.reshape(1, SLOTS), *staged)

    def hand_over(pair_ref, atoms_ref, pair_to, atoms_to, pair_held, atoms_held, loaded, stored):
        parts = [(pair_ref.at[pl.ds(k * 8, 8)], pair_held.at[pl.ds(k * 8, 8)], pair_to.at[pl.ds(k * 8, 8)])
                 for k in range(4)] + [(atoms_ref, atoms_held, atoms_to)]
        loads = [pltpu.make_async_copy(a, b, loaded.at[k]) for k, (a, b, _) in enumerate(parts)]
        stores = [pltpu.make_async_copy(b, c, stored.at[k]) for k, (_, b, c) in enumerate(parts)]
        for load in loads:
            load.start()
        for load, store in zip(loads, stores):
            load.wait()
            store.start()
        for store in stores:
            store.wait()

    hbm = pl.BlockSpec(memory_space=pl.ANY)
    return pl.pallas_call(
        hand_over,
        out_shape=(
            jax.ShapeDtypeStruct(pair_in.shape, bf16),
            jax.ShapeDtypeStruct(atoms_in.shape, bf16),
        ),
        in_specs=[hbm] * 2,
        out_specs=(hbm, hbm),
        scratch_shapes=[
            pltpu.VMEM(pair_in.shape, bf16),
            pltpu.VMEM(atoms_in.shape, bf16),
            pltpu.SemaphoreType.DMA((5,)),
            pltpu.SemaphoreType.DMA((5,)),
        ],
        compiler_params=pltpu.CompilerParams(vmem_limit_bytes=60 * 1024 * 1024),
        name="hand_over",
    )(pair_out, atoms_out)


def solution(mesh):
    placed = (
        P("row", "col", None),
        P(("row", "col"), None),
        P(("row", "col")),
        P(("row", "col")),
        P(),
        P(),
        P(),
        P(),
        P(),
        P(),
        P(),
        P(),
        P(),
    )
    return jax.shard_map(
        body,
        mesh=mesh,
        in_specs=placed,
        out_specs=(P("row", "col", None), P(("row", "col"), None)),
        check_vma=False,
    )
```

```python
import jax
import jax.numpy as jnp
from jax import lax
from jax.experimental import pallas as pl
from jax.experimental.pallas import tpu as pltpu
from jax.sharding import PartitionSpec as P

HEADS = 4
QWIN = 32
KWIN = 128
SIDE = 48
SLOTS = 96
WIDE = SLOTS + 2 * SIDE
START = 2048
EDGE = 2048
CLOSE = 2048
LAST = 1024
ROWS = 16

epsilon = 1e-05

def _far_first():
    shifts = [(x, y, z) for x in range(4) for y in range(4) for z in range(4)][1:]
    return sorted(shifts, key=lambda shift: -sum(min(s, 4 - s) for s in shift))


def _chips(r, c):
    z, y, x = r // 4, lax.rem(c, 2) * 2 + lax.rem(r // 2, 2), c // 2
    xs, ys, zs = [[lax.rem(v + s, 4) for s in range(4)] for v in (x, y, z)]
    row_y = [lax.rem(v, 2) * 2 for v in ys]
    col_y = [v // 2 for v in ys]

    def chip(dx, dy, dz):
        row = zs[dz] * 4 + row_y[dy]
        return row, xs[dx] * 2 + col_y[dy], xs[dx] * 8 + ys[dy] * 2 + zs[dz] // 2

    others = [chip(*shift) + (sum(shift) % 2,) for shift in _far_first()]
    return chip(0, 0, 0)[2], lax.rem(x + y + z, 2), others


def _sigmoid(x):
    return 0.5 * jnp.tanh(0.5 * x) + 0.5


def _norm(x):
    center = x - jnp.mean(x, 0, keepdims=True)
    spread = jnp.mean(center * center, 0, keepdims=True)
    return center * lax.rsqrt(spread + epsilon)


def _dot(a, b):
    return jnp.dot(a, b, preferred_element_type=jnp.float32)


def _flip(x):
    return jnp.transpose(x.astype(jnp.float32)).astype(jnp.bfloat16)


def _norm_rows(x):
    center = x - jnp.mean(x, -1, keepdims=True)
    spread = jnp.mean(center * center, -1, keepdims=True)
    return center * lax.rsqrt(spread + epsilon)


def _ones_where(condition):
    return jnp.where(condition, 1.0, 0.0).astype(jnp.bfloat16)


def _kernel(
    token_ref, mask_ref, *refs,
):
    sources, refs = refs[:11], refs[11:]
    result_ref, atoms_out_ref, *refs = refs
    staged, refs = refs[:11], refs[11:]
    (pair_ref, atoms_ref, atom_w_ref, atom_tin_ref, atom_tout_ref,
     token_in_ref, token_out_ref, out_w_ref, in_w_ref, tin_ref, tout_ref) = staged
    (    state, normed, gate, rows32, weights, tin_t, tout_t,
    send_e, recv_e, edge32, send_p, recv_p, mat_l, mat_r, mat_p,
    halo_out, halo_in, flags, live_token, any_token, wide, mid, featured,
    send_t, recv_t, share, recv_row, recv_right, spreader, add32, added_rows, recv_add,
    sent, got, entered, loaded) = refs
    r = lax.axis_index("row")
    c = lax.axis_index("col")
    me = r * 8 + c
    spot, parity, chips = _chips(r, c)
    core = lax.rem(r, 2)
    sibling = r + 1 - 2 * core
    channel = core * 64 + parity * 32 + spot
    sibling_channel = (1 - core) * 64 + parity * 32 + spot
    barrier = pltpu.get_barrier_semaphore()
    after = lax.rem(me + 1, 128)
    before = lax.rem(me + 127, 128)

    def greet(semaphore, row, col):
        pl.semaphore_signal(
            semaphore, inc=1, device_id=(row, col), device_id_type=pl.DeviceIdType.MESH
        )

    def copy(source, target, k, row, col):
        pltpu.make_async_remote_copy(
            src_ref=source,
            dst_ref=target,
            send_sem=sent.at[k],
            recv_sem=got.at[k],
            device_id=(row, col),
            device_id_type=pl.DeviceIdType.MESH,
        ).start()

    def await_bytes(ref, semaphore):
        pltpu.make_async_copy(ref, ref, semaphore).wait()

    greet(barrier, after // 8, lax.rem(after, 8))
    greet(barrier, before // 8, lax.rem(before, 8))
    for step in range(1, 8):
        greet(barrier, r, lax.rem(c + step, 8))
    for step in range(1, 16):
        greet(barrier, lax.rem(r + step, 16), c)

    loads = [
        pltpu.make_async_copy(source, place, loaded.at[k])
        for k, (source, place) in enumerate(zip(sources, staged))
    ]
    for k in (1, 2, 3, 4, 5, 6, 0, 7, 8, 9, 10):
        loads[k].start()

    flags[...] = jnp.zeros_like(flags)
    flags[:, :SLOTS] = jnp.broadcast_to(
        jnp.where(mask_ref[...] == 1, 1.0, 0.0), (16, SLOTS)
    )
    featured[0] = jnp.zeros((128, 512), jnp.bfloat16)
    featured[0, :SLOTS, 384:] = jnp.ones((SLOTS, 128), jnp.bfloat16)
    any_token[...] = jnp.full_like(any_token, -1)
    any_token[:, :SLOTS] = jnp.broadcast_to(token_ref[...], (8, SLOTS))
    own_flags = flags[...].astype(jnp.bfloat16)
    loads[1].wait()
    halo_out[0, :SIDE] = atoms_ref[SLOTS - SIDE :]
    halo_out[1, :SIDE] = atoms_ref[:SIDE]
    halo_out[0, SIDE:] = own_flags
    halo_out[1, SIDE:] = own_flags
    live_token[0] = jnp.where(flags[:8] > 0.5, any_token[...], -1)
    pl.semaphore_wait(barrier, 24)
    copy(halo_out.at[0], halo_in.at[0], 6, after // 8, lax.rem(after, 8))
    copy(halo_out.at[1], halo_in.at[1], 7, before // 8, lax.rem(before, 8))
    for step in range(1, 16):
        greet(entered, lax.rem(r + step, 16), c)

    own = atoms_ref[...].astype(jnp.float32)
    own_normed = _norm_rows(own).astype(jnp.bfloat16)
    wide[SIDE : SIDE + SLOTS] = own_normed
    loads[2].wait()
    queries = _dot(own_normed, atom_w_ref[0]).astype(jnp.bfloat16)
    atom_gate = _sigmoid(_dot(own_normed, atom_w_ref[3]))
    for k in (6, 7):
        await_bytes(halo_out.at[k - 6], sent.at[k])
        await_bytes(halo_in.at[k - 6], got.at[k])
    wide[:SIDE] = _norm_rows(halo_in[0, :SIDE].astype(jnp.float32)).astype(jnp.bfloat16)
    wide[SIDE + SLOTS :] = _norm_rows(halo_in[1, :SIDE].astype(jnp.float32)).astype(jnp.bfloat16)
    keys = _dot(wide[...], atom_w_ref[1]).astype(jnp.bfloat16)
    values = _dot(wide[...], atom_w_ref[2]).astype(jnp.bfloat16)
    slot = lax.broadcasted_iota(jnp.int32, (128, WIDE), 0)
    key = lax.broadcasted_iota(jnp.int32, (128, WIDE), 1)
    keep = (
        _dot(halo_in[0, SIDE:], _ones_where((key + SIDE == slot) & (me > 0)))
        + _dot(own_flags, _ones_where(key - SIDE == slot))
        + _dot(halo_in[1, SIDE:], _ones_where((key - SIDE - SLOTS == slot) & (me < 127)))
    )[:1]
    query = lax.broadcasted_iota(jnp.int32, (SLOTS, WIDE), 0)
    key = lax.broadcasted_iota(jnp.int32, (SLOTS, WIDE), 1)
    offset = key - (query // QWIN) * QWIN
    inside = (offset >= 0) & (offset < KWIN)
    allowed = jnp.where(inside & ((keep > 0.5) | (key - SIDE == query)), 1.0, 0.0)
    lane_head = lax.broadcasted_iota(jnp.int32, (SLOTS, 128), 1) // 32
    stacked = jnp.concatenate(
        [jnp.where(lane_head == h, queries.astype(jnp.float32), 0.0) for h in range(HEADS)], 0
    ).astype(jnp.bfloat16)
    scores = (
        lax.dot_general(
            stacked, keys, (((1,), (1,)), ((), ())), preferred_element_type=jnp.float32
        )
        * 32**-0.5
    )
    raw = jnp.where(jnp.concatenate([allowed] * HEADS, 0) > 0.5, jnp.exp(scores), 0.0)
    attention = (raw / jnp.sum(raw, -1, keepdims=True)).astype(jnp.bfloat16)
    spread = _dot(attention, values)
    attended = jnp.zeros((SLOTS, 128), jnp.float32)
    for h in range(HEADS):
        attended = attended + jnp.where(lane_head == h, spread[h * SLOTS : (h + 1) * SLOTS], 0.0)
    gated = (atom_gate * attended).astype(jnp.bfloat16)
    resid = own + _dot(gated, atom_w_ref[4])
    resid_normed = _norm_rows(resid).astype(jnp.bfloat16)
    for k in (3, 4, 5):
        loads[k].wait()
    up = _dot(resid_normed, atom_tin_ref[0])
    hidden = (up * _sigmoid(up) * _dot(resid_normed, atom_tin_ref[1])).astype(jnp.bfloat16)
    atom_mid = resid + _dot(hidden, atom_tout_ref[...])
    mid[...] = atom_mid
    feature = jnp.maximum(_dot(atom_mid.astype(jnp.bfloat16), token_in_ref[...]), 0.0)
    featured[0, :SLOTS, :384] = feature.astype(jnp.bfloat16)
    copy(featured.at[0], featured.at[1], 8, sibling, c)
    copy(live_token.at[0], live_token.at[1], 9, sibling, c)

    await_bytes(featured.at[0], sent.at[8])
    await_bytes(live_token.at[0], sent.at[9])
    await_bytes(featured.at[1], got.at[8])
    await_bytes(live_token.at[1], got.at[9])
    slots_token = jnp.concatenate([live_token[0, :1], live_token[1, :1]], 1)
    both = featured[...].reshape(256, 512)
    place = lax.broadcasted_iota(jnp.int32, (64, 256), 0)
    owner = place // 8 * 16 + core * 8 + place % 8
    for t in range(4):
        sums = _dot(_ones_where(owner * 4 + t == slots_token), both)
        for m in range(4):
            rows32[pl.ds(4 * m + t, 64, stride=16), :] = sums[:, m * 128 : (m + 1) * 128]

    def pack(target, first, count):
        target[first : first + count] = (
            rows32[first * 16 : (first + count) * 16].reshape(count, 16, 128).astype(jnp.bfloat16)
        )

    def launch(source, target, k, slot):
        target[slot] = source[me]
        for half in range(2):
            for row, col, _, _ in chips:
                copy(source.at[row * 8 + half * 8 + col], target.at[slot], k, row + half, col)
        copy(source.at[sibling * 8 + c], target.at[slot], k, sibling, c)

    def launch_quarter(source, target, k, half, turn):
        first = half * 64 + lax.rem(parity + turn, 2) * 32
        for row, col, place, shift_parity in chips:
            if shift_parity == turn:
                copy(source.at[first + place], target.at[me], k, row + half, col)

    def finish_copies(source, target, k):
        part = pl.ds(0, 127)
        await_bytes(source.at[part], sent.at[k])
        await_bytes(target.at[part], got.at[k])

    pack(send_t, 0, 64)
    pl.semaphore_wait(entered, 15)
    chip_place = (r // 2) * 8 + c
    recv_t[chip_place] = send_t[chip_place]
    for row, col, _, _ in chips:
        copy(send_t.at[row * 4 + col], recv_t.at[chip_place], 12, row + core, col)

    for k in range(7, 11):
        loads[k].wait()
    for t, source in enumerate((out_w_ref, in_w_ref)):
        for w in range(4):
            turned = _flip(source[w])
            for quarter in range(4):
                place = t * 768 + quarter * 128 + w * 32
                weights[place : place + 32] = turned[quarter * 32 : quarter * 32 + 32]
        for w in (4, 5):
            weights[t * 768 + w * 128 : t * 768 + w * 128 + 128] = _flip(source[w])
    for w in range(2):
        tin_t[w * 512 : w * 512 + 512] = _flip(tin_ref[w])
    tout_t[...] = _flip(tout_ref[...])
    loads[0].wait()
    for a in range(16):
        natural = jnp.concatenate([pair_ref[a], pair_ref[a + 16]], 0).astype(jnp.float32)
        state[:, a * 128 : a * 128 + 128] = jnp.transpose(natural)
        row = lax.broadcasted_iota(jnp.int32, (128, 128), 0)
        lane = lax.broadcasted_iota(jnp.int32, (128, 128), 1)
        right_token = jnp.where(row % 8 >= 4, row // 8 * 4 + row % 8 - 4, -1)
        spreader[:128, a * 128 : a * 128 + 128] = _ones_where(lane % 64 == right_token)
        left_token = jnp.where(row % 16 < 4, row // 16 * 4 + row % 16, -1)
        spreader[128:, a * 128 : a * 128 + 128] = _ones_where(
            jnp.where(lane < 64, a, a + 16) == left_token
        )
    loads[6].wait()
    await_bytes(send_t.at[pl.ds(0, 63)], sent.at[12])
    await_bytes(recv_t.at[pl.ds(0, 63)], got.at[12])

    total = jnp.zeros((16, 128), jnp.float32)
    for d in range(0, 64, 32):
        total = total + jnp.sum(recv_t[d : d + 32].astype(jnp.float32), 0)
    count = jnp.maximum(total[12:], 1.0)
    single = jnp.concatenate([total[4 * m : 4 * m + 4] / count for m in range(3)], 1)
    proj = _dot(single.astype(jnp.bfloat16), token_out_ref[...])
    share[...] = jnp.zeros_like(share)
    for m in range(3):
        share[4 * m : 4 * m + 4] = proj[:, m * 128 : (m + 1) * 128]

    recv_row[c] = share[...]
    column = me // 16
    place = lax.rem(me, 16)
    for step in range(1, 16):
        row = lax.rem(r + step, 16)
        copy(share.at[pl.ds(0, 8)], recv_right.at[place], 10, row, column)

    @pl.when(column == c)
    def _():
        recv_right[place] = share[pl.ds(0, 8)]

    @pl.when(column != c)
    def _():
        copy(share.at[pl.ds(0, 8)], recv_right.at[place], 10, r, column)

    for step in range(1, 8):
        copy(share, recv_row.at[c], 13, r, lax.rem(c + step, 8))

    @pl.when(column != c)
    def _():
        await_bytes(recv_right.at[pl.ds(0, 1)], sent.at[10])

    await_bytes(recv_right.at[pl.ds(0, 15)], sent.at[10])
    await_bytes(recv_row.at[pl.ds(0, 7)], sent.at[13])

    mine = (me >= 16 * c) & (me < 16 * c + 16)

    @pl.when(mine)
    def _():
        await_bytes(recv_right.at[pl.ds(0, 15)], got.at[10])

    @pl.when(jnp.logical_not(mine))
    def _():
        await_bytes(recv_right, got.at[10])

    await_bytes(recv_row.at[pl.ds(0, 7)], got.at[13])
    def spans(width, step):
        if width == 2048:
            step(0)
        else:
            lax.fori_loop(0, 2048 // width, lambda g, _: (step(g), 0)[1], 0)

    def lanes(g, width):
        return pl.ds(g * width if isinstance(g, int) else pl.multiple_of(g * width, width), width)

    over_rows = (((0,), (0,)), ((), ()))
    rows = jnp.concatenate(
        [recv_right[...].reshape(128, 128), recv_row[...].reshape(128, 128)], 0
    )
    high = rows.astype(jnp.bfloat16)
    low = (rows - high.astype(jnp.float32)).astype(jnp.bfloat16)

    def start_state(g):
        here = lanes(g, START)
        spread = spreader[:, here]
        started = (
            state[:, here]
            + lax.dot_general(high, spread, over_rows, preferred_element_type=jnp.float32)
            + lax.dot_general(low, spread, over_rows, preferred_element_type=jnp.float32)
        )
        state[:, here] = started
        normed[:, here] = _norm(started).astype(jnp.bfloat16)

    spans(START, start_state)

    def edges(t, half, turn, target):
        quarter = half * 2 + lax.rem(parity + turn, 2)
        stage = (half * 2 + turn) * 1024
        place = pl.ds(pl.multiple_of(t * 768 + quarter * 128, 128), 128)

        def chunk(g):
            both = _dot(weights[place, :], normed[:, lanes(g, EDGE)])
            left = _sigmoid(both[:32]) * both[32:64]
            right = _sigmoid(both[64:96]) * both[96:]
            for h in range(EDGE // 128):
                a = stage + g * (EDGE // 128) + h
                part = slice(h * 128, h * 128 + 128)
                edge32[pl.ds(a, 32, stride=32), :] = left[:, part]
                edge32[pl.ds(a + 16, 32, stride=32), :] = right[:, part]

        spans(EDGE, chunk)
        target[pl.ds(quarter * 32, 32)] = (
            edge32[stage : stage + 1024].reshape(32, 32, 128).astype(jnp.bfloat16)
        )

    def gates(base):
        def chunk(g):
            gate[:, lanes(g, EDGE)] = _sigmoid(
                _dot(weights[pl.ds((base + 4) * 128, 128), :], normed[:, lanes(g, EDGE)])
            )

        spans(EDGE, chunk)

    low_lanes = lax.broadcasted_iota(jnp.int32, (16, 128), 1) < 64

    def assemble(source, first, target):
        def block(g, _):
            for k in range(ROWS):
                row = g * ROWS + k
                for q in range(4):
                    even = source[row * 8 + 2 * q, first : first + 16]
                    odd = source[row * 8 + 2 * q + 1, first : first + 16]
                    target[pl.ds(row * 32, 16), pl.ds(q * 128, 128)] = jnp.where(
                        low_lanes, even, pltpu.roll(odd, 64, 1)
                    )
                    target[pl.ds(row * 32 + 16, 16), pl.ds(q * 128, 128)] = jnp.where(
                        low_lanes, pltpu.roll(even, 64, 1), odd
                    )
            return 0

        lax.fori_loop(0, 16 // ROWS, block, 0)

    def split(source, target):
        def block(g, _):
            for k in range(ROWS):
                row = g * ROWS + k
                for q in range(4):
                    top = source[pl.ds(row * 32, 16), pl.ds(q * 128, 128)]
                    low = source[pl.ds(row * 32 + 16, 16), pl.ds(q * 128, 128)]
                    target[row * 8 + 2 * q] = jnp.where(low_lanes, top, pltpu.roll(low, 64, 1))
                    target[row * 8 + 2 * q + 1] = jnp.where(low_lanes, pltpu.roll(top, 64, 1), low)
            return 0

        lax.fori_loop(0, 16 // ROWS, block, 0)

    def triangle(t, width, beside, after):
        base = 6 * t
        for half in range(2):
            for turn in range(2):
                edges(t, half, turn, send_e.at[t])
                launch_quarter(send_e.at[t], recv_e.at[t], 2 * t, half, turn)
        copy(send_e.at[t, sibling_channel], recv_e.at[t, me], 2 * t, sibling, c)
        recv_e[t, me] = send_e[t, channel]
        gates(base)
        finish_copies(send_e.at[t], recv_e.at[t], 2 * t)
        if t == 1:
            for step in range(1, 16):
                copy(added_rows, recv_add.at[r], 11, lax.rem(r + step, 16), c)
        assemble(recv_e.at[t], 0, mat_l)
        assemble(recv_e.at[t], 16, mat_r)
        axis = 1 - t
        mat_p[...] = lax.dot_general(
            mat_l[...],
            mat_r[...],
            (((axis,), (axis,)), ((), ())),
            preferred_element_type=jnp.float32,
        ).astype(jnp.bfloat16)
        split(mat_p, send_p.at[t])
        launch(send_p.at[t], recv_p.at[t], 2 * t + 1, channel)
        beside()
        finish_copies(send_p.at[t], recv_p.at[t], 2 * t + 1)

        rows32[...] = recv_p[t].astype(jnp.float32).reshape(2048, 128)

        def close(g):
            count = width // 128
            product = jnp.concatenate(
                [rows32[pl.ds(g * count + h, 128, stride=16), :] for h in range(count)], 1
            )
            product = _norm(product).astype(jnp.bfloat16)
            here = lanes(g, width)
            updated = state[:, here] + gate[:, here] * _dot(
                weights[pl.ds((base + 5) * 128, 128), :], product
            )
            after(g, width, updated)

        spans(width, close)

    def next_update(g, width, updated):
        state[:, lanes(g, width)] = updated
        normed[:, lanes(g, width)] = _norm(updated).astype(jnp.bfloat16)

    def transition(g, width, updated):
        inner = _dot(tin_t[...], _norm(updated).astype(jnp.bfloat16))
        up = inner[:512]
        hidden = (up * _sigmoid(up) * inner[512:]).astype(jnp.bfloat16)
        final = updated + _dot(tout_t[...], hidden)
        for h in range(width // 128):
            natural = jnp.transpose(final[:, h * 128 : (h + 1) * 128]).astype(jnp.bfloat16)
            result_ref[g * (width // 128) + h] = natural[:64]
            result_ref[g * (width // 128) + h + 16] = natural[64:]

    def share_added():
        for j in range(8):
            add32[4 * j : 4 * j + 4] = recv_row[j, 8:12]
        added_rows[...] = add32[...].astype(jnp.bfloat16)
        recv_add[r] = added_rows[...]

    def finish_atoms():
        await_bytes(recv_add.at[pl.ds(0, 15)], sent.at[11])
        await_bytes(recv_add.at[pl.ds(0, 15)], got.at[11])
        token = lax.broadcasted_iota(jnp.int32, (512, 128), 0)
        chosen = _ones_where(token == any_token[:1])
        picked = lax.dot_general(
            chosen,
            recv_add[...].reshape(512, 128),
            over_rows,
            preferred_element_type=jnp.float32,
        )
        atoms_out_ref[...] = (mid[...] + picked[:SLOTS]).astype(jnp.bfloat16)

    triangle(0, CLOSE, share_added, next_update)
    triangle(1, LAST, finish_atoms, transition)


def body(pair_in, atoms_in, atom_token, atom_mask, *parameters):
    vmem = pl.BlockSpec(memory_space=pltpu.VMEM)
    staged = (pair_in, atoms_in, *parameters)
    bf16, f32 = jnp.bfloat16, jnp.float32
    pair_out, atoms_out = pl.pallas_call(
        _kernel,
        out_shape=(
            jax.ShapeDtypeStruct(pair_in.shape, bf16),
            jax.ShapeDtypeStruct(atoms_in.shape, bf16),
        ),
        in_specs=[vmem] * 2 + [pl.BlockSpec(memory_space=pltpu.HBM)] * 11,
        out_specs=(vmem, vmem),
        scratch_shapes=[pltpu.VMEM(array.shape, array.dtype) for array in staged]
        + [
            pltpu.VMEM((128, 2048), f32),
            pltpu.VMEM((128, 2048), bf16),
            pltpu.VMEM((128, 2048), f32),
            pltpu.VMEM((2048, 128), f32),
            pltpu.VMEM((1536, 128), bf16),
            pltpu.VMEM((1024, 128), bf16),
            pltpu.VMEM((128, 512), bf16),
        ]
        + [pltpu.VMEM((2, 128, 32, 128), bf16)] * 2
        + [pltpu.VMEM((4096, 128), f32)]
        + [pltpu.VMEM((2, 128, 16, 128), bf16)] * 2
        + [pltpu.VMEM((512, 512), bf16)] * 3
        + [
            pltpu.VMEM((2, 64, 128), bf16),
            pltpu.VMEM((2, 64, 128), bf16),
            pltpu.VMEM((16, 128), f32),
            pltpu.VMEM((2, 8, 128), jnp.int32),
            pltpu.VMEM((8, 128), jnp.int32),
            pltpu.VMEM((WIDE, 128), bf16),
            pltpu.VMEM((SLOTS, 128), f32),
            pltpu.VMEM((2, 128, 512), bf16),
            pltpu.VMEM((64, 16, 128), bf16),
            pltpu.VMEM((64, 16, 128), bf16),
            pltpu.VMEM((16, 128), f32),
            pltpu.VMEM((8, 16, 128), f32),
            pltpu.VMEM((16, 8, 128), f32),
            pltpu.VMEM((256, 2048), bf16),
            pltpu.VMEM((32, 128), f32),
            pltpu.VMEM((32, 128), bf16),
            pltpu.VMEM((16, 32, 128), bf16),
            pltpu.SemaphoreType.DMA((14,)),
            pltpu.SemaphoreType.DMA((14,)),
            pltpu.SemaphoreType.REGULAR,
            pltpu.SemaphoreType.DMA((11,)),
        ],
        compiler_params=pltpu.CompilerParams(
            collective_id=0, has_side_effects=True, vmem_limit_bytes=60 * 1024 * 1024
        ),
        name="atoms_and_pair",
    )(atom_token.reshape(1, SLOTS), atom_mask.reshape(1, SLOTS), *staged)

    def hand_over(pair_ref, atoms_ref, pair_to, atoms_to, pair_held, atoms_held, loaded, stored):
        parts = [(pair_ref.at[pl.ds(k * 8, 8)], pair_held.at[pl.ds(k * 8, 8)], pair_to.at[pl.ds(k * 8, 8)])
                 for k in range(4)] + [(atoms_ref, atoms_held, atoms_to)]
        loads = [pltpu.make_async_copy(a, b, loaded.at[k]) for k, (a, b, _) in enumerate(parts)]
        stores = [pltpu.make_async_copy(b, c, stored.at[k]) for k, (_, b, c) in enumerate(parts)]
        for load in loads:
            load.start()
        for load, store in zip(loads, stores):
            load.wait()
            store.start()
        for store in stores:
            store.wait()

    hbm = pl.BlockSpec(memory_space=pl.ANY)
    return pl.pallas_call(
        hand_over,
        out_shape=(
            jax.ShapeDtypeStruct(pair_in.shape, bf16),
            jax.ShapeDtypeStruct(atoms_in.shape, bf16),
        ),
        in_specs=[hbm] * 2,
        out_specs=(hbm, hbm),
        scratch_shapes=[
            pltpu.VMEM(pair_in.shape, bf16),
            pltpu.VMEM(atoms_in.shape, bf16),
            pltpu.SemaphoreType.DMA((5,)),
            pltpu.SemaphoreType.DMA((5,)),
        ],
        compiler_params=pltpu.CompilerParams(vmem_limit_bytes=60 * 1024 * 1024),
        name="hand_over",
    )(pair_out, atoms_out)


def solution(mesh):
    placed = (
        P("row", "col", None),
        P(("row", "col"), None),
        P(("row", "col")),
        P(("row", "col")),
        P(),
        P(),
        P(),
        P(),
        P(),
        P(),
        P(),
        P(),
        P(),
    )
    return jax.shard_map(
        body,
        mesh=mesh,
        in_specs=placed,
        out_specs=(P("row", "col", None), P(("row", "col"), None)),
        check_vma=False,
    )
```

```python
import jax
import jax.numpy as jnp
from jax import lax
from jax.experimental import pallas as pl
from jax.experimental.pallas import tpu as pltpu
from jax.sharding import PartitionSpec as P

HEADS = 4
QWIN = 32
KWIN = 128
SIDE = 48
SLOTS = 96
WIDE = SLOTS + 2 * SIDE
START = 2048
EDGE = 2048
CLOSE = 2048
LAST = 1024
ROWS = 16

epsilon = 1e-05

def _far_first():
    shifts = [(x, y, z) for x in range(4) for y in range(4) for z in range(4)][1:]
    return sorted(shifts, key=lambda shift: -sum(min(s, 4 - s) for s in shift))


def _chips(r, c):
    z, y, x = r // 4, lax.rem(c, 2) * 2 + lax.rem(r // 2, 2), c // 2
    xs, ys, zs = [[lax.rem(v + s, 4) for s in range(4)] for v in (x, y, z)]
    row_y = [lax.rem(v, 2) * 2 for v in ys]
    col_y = [v // 2 for v in ys]

    def chip(dx, dy, dz):
        row = zs[dz] * 4 + row_y[dy]
        return row, xs[dx] * 2 + col_y[dy], xs[dx] * 8 + ys[dy] * 2 + zs[dz] // 2

    others = [chip(*shift) + (sum(shift) % 2,) for shift in _far_first()]
    return chip(0, 0, 0)[2], lax.rem(x + y + z, 2), others


def _sigmoid(x):
    return 0.5 * jnp.tanh(0.5 * x) + 0.5


def _norm(x):
    center = x - jnp.mean(x, 0, keepdims=True)
    spread = jnp.mean(center * center, 0, keepdims=True)
    return center * lax.rsqrt(spread + epsilon)


def _dot(a, b):
    return jnp.dot(a, b, preferred_element_type=jnp.float32)


def _flip(x):
    return jnp.transpose(x.astype(jnp.float32)).astype(jnp.bfloat16)


def _norm_rows(x):
    center = x - jnp.mean(x, -1, keepdims=True)
    spread = jnp.mean(center * center, -1, keepdims=True)
    return center * lax.rsqrt(spread + epsilon)


def _ones_where(condition):
    return jnp.where(condition, 1.0, 0.0).astype(jnp.bfloat16)


def _kernel(
    token_ref, mask_ref, *refs,
):
    sources, refs = refs[:11], refs[11:]
    result_ref, atoms_out_ref, *refs = refs
    staged, refs = refs[:11], refs[11:]
    (pair_ref, atoms_ref, atom_w_ref, atom_tin_ref, atom_tout_ref,
     token_in_ref, token_out_ref, out_w_ref, in_w_ref, tin_ref, tout_ref) = staged
    (    state, normed, gate, rows32, weights, tin_t, tout_t,
    send_e, recv_e, edge32, send_p, recv_p, mat_l, mat_r, mat_p,
    halo_out, halo_in, flags, live_token, any_token, wide, mid, featured,
    send_t, recv_t, share, recv_row, recv_right, spreader, add32, added_rows, recv_add,
    sent, got, entered, loaded) = refs
    r = lax.axis_index("row")
    c = lax.axis_index("col")
    me = r * 8 + c
    spot, parity, chips = _chips(r, c)
    core = lax.rem(r, 2)
    sibling = r + 1 - 2 * core
    channel = core * 64 + parity * 32 + spot
    sibling_channel = (1 - core) * 64 + parity * 32 + spot
    barrier = pltpu.get_barrier_semaphore()
    after = lax.rem(me + 1, 128)
    before = lax.rem(me + 127, 128)

    def greet(semaphore, row, col):
        pl.semaphore_signal(
            semaphore, inc=1, device_id=(row, col), device_id_type=pl.DeviceIdType.MESH
        )

    def copy(source, target, k, row, col):
        pltpu.make_async_remote_copy(
            src_ref=source,
            dst_ref=target,
            send_sem=sent.at[k],
            recv_sem=got.at[k],
            device_id=(row, col),
            device_id_type=pl.DeviceIdType.MESH,
        ).start()

    def await_bytes(ref, semaphore):
        pltpu.make_async_copy(ref, ref, semaphore).wait()

    greet(barrier, after // 8, lax.rem(after, 8))
    greet(barrier, before // 8, lax.rem(before, 8))
    for step in range(1, 8):
        greet(barrier, r, lax.rem(c + step, 8))
    for step in range(1, 16):
        greet(barrier, lax.rem(r + step, 16), c)

    loads = [
        pltpu.make_async_copy(source, place, loaded.at[k])
        for k, (source, place) in enumerate(zip(sources, staged))
    ]
    for k in (1, 2, 3, 4, 5, 6, 0, 7, 8, 9, 10):
        loads[k].start()

    flags[...] = jnp.zeros_like(flags)
    flags[:, :SLOTS] = jnp.broadcast_to(
        jnp.where(mask_ref[...] == 1, 1.0, 0.0), (16, SLOTS)
    )
    featured[0] = jnp.zeros((128, 512), jnp.bfloat16)
    featured[0, :SLOTS, 384:] = jnp.ones((SLOTS, 128), jnp.bfloat16)
    any_token[...] = jnp.full_like(any_token, -1)
    any_token[:, :SLOTS] = jnp.broadcast_to(token_ref[...], (8, SLOTS))
    own_flags = flags[...].astype(jnp.bfloat16)
    loads[1].wait()
    halo_out[0, :SIDE] = atoms_ref[SLOTS - SIDE :]
    halo_out[1, :SIDE] = atoms_ref[:SIDE]
    halo_out[0, SIDE:] = own_flags
    halo_out[1, SIDE:] = own_flags
    live_token[0] = jnp.where(flags[:8] > 0.5, any_token[...], -1)
    pl.semaphore_wait(barrier, 24)
    copy(halo_out.at[0], halo_in.at[0], 6, after // 8, lax.rem(after, 8))
    copy(halo_out.at[1], halo_in.at[1], 7, before // 8, lax.rem(before, 8))
    for step in range(1, 16):
        greet(entered, lax.rem(r + step, 16), c)

    own = atoms_ref[...].astype(jnp.float32)
    own_normed = _norm_rows(own).astype(jnp.bfloat16)
    wide[SIDE : SIDE + SLOTS] = own_normed
    loads[2].wait()
    queries = _dot(own_normed, atom_w_ref[0]).astype(jnp.bfloat16)
    atom_gate = _sigmoid(_dot(own_normed, atom_w_ref[3]))
    for k in (6, 7):
        await_bytes(halo_out.at[k - 6], sent.at[k])
        await_bytes(halo_in.at[k - 6], got.at[k])
    wide[:SIDE] = _norm_rows(halo_in[0, :SIDE].astype(jnp.float32)).astype(jnp.bfloat16)
    wide[SIDE + SLOTS :] = _norm_rows(halo_in[1, :SIDE].astype(jnp.float32)).astype(jnp.bfloat16)
    keys = _dot(wide[...], atom_w_ref[1]).astype(jnp.bfloat16)
    values = _dot(wide[...], atom_w_ref[2]).astype(jnp.bfloat16)
    slot = lax.broadcasted_iota(jnp.int32, (128, WIDE), 0)
    key = lax.broadcasted_iota(jnp.int32, (128, WIDE), 1)
    keep = (
        _dot(halo_in[0, SIDE:], _ones_where((key + SIDE == slot) & (me > 0)))
        + _dot(own_flags, _ones_where(key - SIDE == slot))
        + _dot(halo_in[1, SIDE:], _ones_where((key - SIDE - SLOTS == slot) & (me < 127)))
    )[:1]
    query = lax.broadcasted_iota(jnp.int32, (SLOTS, WIDE), 0)
    key = lax.broadcasted_iota(jnp.int32, (SLOTS, WIDE), 1)
    offset = key - (query // QWIN) * QWIN
    inside = (offset >= 0) & (offset < KWIN)
    allowed = jnp.where(inside & ((keep > 0.5) | (key - SIDE == query)), 1.0, 0.0)
    lane_head = lax.broadcasted_iota(jnp.int32, (SLOTS, 128), 1) // 32
    stacked = jnp.concatenate(
        [jnp.where(lane_head == h, queries.astype(jnp.float32), 0.0) for h in range(HEADS)], 0
    ).astype(jnp.bfloat16)
    scores = (
        lax.dot_general(
            stacked, keys, (((1,), (1,)), ((), ())), preferred_element_type=jnp.float32
        )
        * 32**-0.5
    )
    raw = jnp.where(jnp.concatenate([allowed] * HEADS, 0) > 0.5, jnp.exp(scores), 0.0)
    attention = (raw / jnp.sum(raw, -1, keepdims=True)).astype(jnp.bfloat16)
    spread = _dot(attention, values)
    attended = jnp.zeros((SLOTS, 128), jnp.float32)
    for h in range(HEADS):
        attended = attended + jnp.where(lane_head == h, spread[h * SLOTS : (h + 1) * SLOTS], 0.0)
    gated = (atom_gate * attended).astype(jnp.bfloat16)
    resid = own + _dot(gated, atom_w_ref[4])
    resid_normed = _norm_rows(resid).astype(jnp.bfloat16)
    for k in (3, 4, 5):
        loads[k].wait()
    up = _dot(resid_normed, atom_tin_ref[0])
    hidden = (up * _sigmoid(up) * _dot(resid_normed, atom_tin_ref[1])).astype(jnp.bfloat16)
    atom_mid = resid + _dot(hidden, atom_tout_ref[...])
    mid[...] = atom_mid
    feature = jnp.maximum(_dot(atom_mid.astype(jnp.bfloat16), token_in_ref[...]), 0.0)
    featured[0, :SLOTS, :384] = feature.astype(jnp.bfloat16)
    copy(featured.at[0], featured.at[1], 8, sibling, c)
    copy(live_token.at[0], live_token.at[1], 9, sibling, c)

    await_bytes(featured.at[0], sent.at[8])
    await_bytes(live_token.at[0], sent.at[9])
    await_bytes(featured.at[1], got.at[8])
    await_bytes(live_token.at[1], got.at[9])
    slots_token = jnp.concatenate([live_token[0, :1], live_token[1, :1]], 1)
    both = featured[...].reshape(256, 512)
    place = lax.broadcasted_iota(jnp.int32, (64, 256), 0)
    owner = place // 8 * 16 + core * 8 + place % 8
    for t in range(4):
        sums = _dot(_ones_where(owner * 4 + t == slots_token), both)
        for m in range(4):
            rows32[pl.ds(4 * m + t, 64, stride=16), :] = sums[:, m * 128 : (m + 1) * 128]

    def pack(target, first, count):
        target[first : first + count] = (
            rows32[first * 16 : (first + count) * 16].reshape(count, 16, 128).astype(jnp.bfloat16)
        )

    def launch(source, target, k, slot):
        target[slot] = source[me]
        for half in range(2):
            for row, col, _, _ in chips:
                copy(source.at[row * 8 + half * 8 + col], target.at[slot], k, row + half, col)
        copy(source.at[sibling * 8 + c], target.at[slot], k, sibling, c)

    def launch_quarter(source, target, k, half, turn):
        first = half * 64 + lax.rem(parity + turn, 2) * 32
        for row, col, place, shift_parity in chips:
            if shift_parity == turn:
                copy(source.at[first + place], target.at[me], k, row + half, col)

    def finish_copies(source, target, k):
        part = pl.ds(0, 127)
        await_bytes(source.at[part], sent.at[k])
        await_bytes(target.at[part], got.at[k])

    pack(send_t, 0, 64)
    pl.semaphore_wait(entered, 15)
    chip_place = (r // 2) * 8 + c
    recv_t[chip_place] = send_t[chip_place]
    for row, col, _, _ in chips:
        copy(send_t.at[row * 4 + col], recv_t.at[chip_place], 12, row + core, col)

    for k in range(7, 11):
        loads[k].wait()
    for t, source in enumerate((out_w_ref, in_w_ref)):
        for w in range(4):
            turned = _flip(source[w])
            for quarter in range(4):
                place = t * 768 + quarter * 128 + w * 32
                weights[place : place + 32] = turned[quarter * 32 : quarter * 32 + 32]
        for w in (4, 5):
            weights[t * 768 + w * 128 : t * 768 + w * 128 + 128] = _flip(source[w])
    for w in range(2):
        tin_t[w * 512 : w * 512 + 512] = _flip(tin_ref[w])
    tout_t[...] = _flip(tout_ref[...])
    loads[0].wait()
    for a in range(16):
        natural = jnp.concatenate([pair_ref[a], pair_ref[a + 16]], 0).astype(jnp.float32)
        state[:, a * 128 : a * 128 + 128] = jnp.transpose(natural)
        row = lax.broadcasted_iota(jnp.int32, (128, 128), 0)
        lane = lax.broadcasted_iota(jnp.int32, (128, 128), 1)
        right_token = jnp.where(row % 8 >= 4, row // 8 * 4 + row % 8 - 4, -1)
        spreader[:128, a * 128 : a * 128 + 128] = _ones_where(lane % 64 == right_token)
        left_token = jnp.where(row % 16 < 4, row // 16 * 4 + row % 16, -1)
        spreader[128:, a * 128 : a * 128 + 128] = _ones_where(
            jnp.where(lane < 64, a, a + 16) == left_token
        )
    loads[6].wait()
    await_bytes(send_t.at[pl.ds(0, 63)], sent.at[12])
    await_bytes(recv_t.at[pl.ds(0, 63)], got.at[12])

    total = jnp.zeros((16, 128), jnp.float32)
    for d in range(0, 64, 32):
        total = total + jnp.sum(recv_t[d : d + 32].astype(jnp.float32), 0)
    count = jnp.maximum(total[12:], 1.0)
    single = jnp.concatenate([total[4 * m : 4 * m + 4] / count for m in range(3)], 1)
    proj = _dot(single.astype(jnp.bfloat16), token_out_ref[...])
    share[...] = jnp.zeros_like(share)
    for m in range(3):
        share[4 * m : 4 * m + 4] = proj[:, m * 128 : (m + 1) * 128]

    recv_row[c] = share[...]
    column = me // 16
    place = lax.rem(me, 16)
    for step in range(1, 16):
        row = lax.rem(r + step, 16)
        copy(share.at[pl.ds(0, 8)], recv_right.at[place], 10, row, column)

    @pl.when(column == c)
    def _():
        recv_right[place] = share[pl.ds(0, 8)]

    @pl.when(column != c)
    def _():
        copy(share.at[pl.ds(0, 8)], recv_right.at[place], 10, r, column)

    for step in range(1, 8):
        copy(share, recv_row.at[c], 13, r, lax.rem(c + step, 8))

    @pl.when(column != c)
    def _():
        await_bytes(recv_right.at[pl.ds(0, 1)], sent.at[10])

    await_bytes(recv_right.at[pl.ds(0, 15)], sent.at[10])
    await_bytes(recv_row.at[pl.ds(0, 7)], sent.at[13])

    mine = (me >= 16 * c) & (me < 16 * c + 16)

    @pl.when(mine)
    def _():
        await_bytes(recv_right.at[pl.ds(0, 15)], got.at[10])

    @pl.when(jnp.logical_not(mine))
    def _():
        await_bytes(recv_right, got.at[10])

    await_bytes(recv_row.at[pl.ds(0, 7)], got.at[13])
    def spans(width, step):
        if width == 2048:
            step(0)
        else:
            lax.fori_loop(0, 2048 // width, lambda g, _: (step(g), 0)[1], 0)

    def lanes(g, width):
        return pl.ds(g * width if isinstance(g, int) else pl.multiple_of(g * width, width), width)

    over_rows = (((0,), (0,)), ((), ()))
    rows = jnp.concatenate(
        [recv_right[...].reshape(128, 128), recv_row[...].reshape(128, 128)], 0
    )
    high = rows.astype(jnp.bfloat16)
    low = (rows - high.astype(jnp.float32)).astype(jnp.bfloat16)

    def start_state(g):
        here = lanes(g, START)
        spread = spreader[:, here]
        started = (
            state[:, here]
            + lax.dot_general(high, spread, over_rows, preferred_element_type=jnp.float32)
            + lax.dot_general(low, spread, over_rows, preferred_element_type=jnp.float32)
        )
        state[:, here] = started
        normed[:, here] = _norm(started).astype(jnp.bfloat16)

    spans(START, start_state)

    def edges(t, half, turn, target):
        quarter = half * 2 + lax.rem(parity + turn, 2)
        stage = (half * 2 + turn) * 1024
        place = pl.ds(pl.multiple_of(t * 768 + quarter * 128, 128), 128)

        def chunk(g):
            both = _dot(weights[place, :], normed[:, lanes(g, EDGE)])
            left = _sigmoid(both[:32]) * both[32:64]
            right = _sigmoid(both[64:96]) * both[96:]
            for h in range(EDGE // 128):
                a = stage + g * (EDGE // 128) + h
                part = slice(h * 128, h * 128 + 128)
                edge32[pl.ds(a, 32, stride=32), :] = left[:, part]
                edge32[pl.ds(a + 16, 32, stride=32), :] = right[:, part]

        spans(EDGE, chunk)
        target[pl.ds(quarter * 32, 32)] = (
            edge32[stage : stage + 1024].reshape(32, 32, 128).astype(jnp.bfloat16)
        )

    def gates(base):
        def chunk(g):
            gate[:, lanes(g, EDGE)] = _sigmoid(
                _dot(weights[pl.ds((base + 4) * 128, 128), :], normed[:, lanes(g, EDGE)])
            )

        spans(EDGE, chunk)

    low_lanes = lax.broadcasted_iota(jnp.int32, (16, 128), 1) < 64

    def assemble(source, first, target):
        def block(g, _):
            for k in range(ROWS):
                row = g * ROWS + k
                for q in range(4):
                    even = source[row * 8 + 2 * q, first : first + 16]
                    odd = source[row * 8 + 2 * q + 1, first : first + 16]
                    target[pl.ds(row * 32, 16), pl.ds(q * 128, 128)] = jnp.where(
                        low_lanes, even, pltpu.roll(odd, 64, 1)
                    )
                    target[pl.ds(row * 32 + 16, 16), pl.ds(q * 128, 128)] = jnp.where(
                        low_lanes, pltpu.roll(even, 64, 1), odd
                    )
            return 0

        lax.fori_loop(0, 16 // ROWS, block, 0)

    def split(source, target):
        def block(g, _):
            for k in range(ROWS):
                row = g * ROWS + k
                for q in range(4):
                    top = source[pl.ds(row * 32, 16), pl.ds(q * 128, 128)]
                    low = source[pl.ds(row * 32 + 16, 16), pl.ds(q * 128, 128)]
                    target[row * 8 + 2 * q] = jnp.where(low_lanes, top, pltpu.roll(low, 64, 1))
                    target[row * 8 + 2 * q + 1] = jnp.where(low_lanes, pltpu.roll(top, 64, 1), low)
            return 0

        lax.fori_loop(0, 16 // ROWS, block, 0)

    def triangle(t, width, beside, after):
        base = 6 * t
        for half in range(2):
            for turn in (1, 0):
                edges(t, half, turn, send_e.at[t])
                launch_quarter(send_e.at[t], recv_e.at[t], 2 * t, half, turn)
        copy(send_e.at[t, sibling_channel], recv_e.at[t, me], 2 * t, sibling, c)
        recv_e[t, me] = send_e[t, channel]
        gates(base)
        finish_copies(send_e.at[t], recv_e.at[t], 2 * t)
        if t == 1:
            for step in range(1, 16):
                copy(added_rows, recv_add.at[r], 11, lax.rem(r + step, 16), c)
        assemble(recv_e.at[t], 0, mat_l)
        assemble(recv_e.at[t], 16, mat_r)
        axis = 1 - t
        mat_p[...] = lax.dot_general(
            mat_l[...],
            mat_r[...],
            (((axis,), (axis,)), ((), ())),
            preferred_element_type=jnp.float32,
        ).astype(jnp.bfloat16)
        split(mat_p, send_p.at[t])
        launch(send_p.at[t], recv_p.at[t], 2 * t + 1, channel)
        beside()
        finish_copies(send_p.at[t], recv_p.at[t], 2 * t + 1)

        rows32[...] = recv_p[t].astype(jnp.float32).reshape(2048, 128)

        def close(g):
            count = width // 128
            product = jnp.concatenate(
                [rows32[pl.ds(g * count + h, 128, stride=16), :] for h in range(count)], 1
            )
            product = _norm(product).astype(jnp.bfloat16)
            here = lanes(g, width)
            updated = state[:, here] + gate[:, here] * _dot(
                weights[pl.ds((base + 5) * 128, 128), :], product
            )
            after(g, width, updated)

        spans(width, close)

    def next_update(g, width, updated):
        state[:, lanes(g, width)] = updated
        normed[:, lanes(g, width)] = _norm(updated).astype(jnp.bfloat16)

    def transition(g, width, updated):
        inner = _dot(tin_t[...], _norm(updated).astype(jnp.bfloat16))
        up = inner[:512]
        hidden = (up * _sigmoid(up) * inner[512:]).astype(jnp.bfloat16)
        final = updated + _dot(tout_t[...], hidden)
        for h in range(width // 128):
            natural = jnp.transpose(final[:, h * 128 : (h + 1) * 128]).astype(jnp.bfloat16)
            result_ref[g * (width // 128) + h] = natural[:64]
            result_ref[g * (width // 128) + h + 16] = natural[64:]

    def share_added():
        for j in range(8):
            add32[4 * j : 4 * j + 4] = recv_row[j, 8:12]
        added_rows[...] = add32[...].astype(jnp.bfloat16)
        recv_add[r] = added_rows[...]

    def finish_atoms():
        await_bytes(recv_add.at[pl.ds(0, 15)], sent.at[11])
        await_bytes(recv_add.at[pl.ds(0, 15)], got.at[11])
        token = lax.broadcasted_iota(jnp.int32, (512, 128), 0)
        chosen = _ones_where(token == any_token[:1])
        picked = lax.dot_general(
            chosen,
            recv_add[...].reshape(512, 128),
            over_rows,
            preferred_element_type=jnp.float32,
        )
        atoms_out_ref[...] = (mid[...] + picked[:SLOTS]).astype(jnp.bfloat16)

    triangle(0, CLOSE, share_added, next_update)
    triangle(1, LAST, finish_atoms, transition)


def body(pair_in, atoms_in, atom_token, atom_mask, *parameters):
    vmem = pl.BlockSpec(memory_space=pltpu.VMEM)
    staged = (pair_in, atoms_in, *parameters)
    bf16, f32 = jnp.bfloat16, jnp.float32
    pair_out, atoms_out = pl.pallas_call(
        _kernel,
        out_shape=(
            jax.ShapeDtypeStruct(pair_in.shape, bf16),
            jax.ShapeDtypeStruct(atoms_in.shape, bf16),
        ),
        in_specs=[vmem] * 2 + [pl.BlockSpec(memory_space=pltpu.HBM)] * 11,
        out_specs=(vmem, vmem),
        scratch_shapes=[pltpu.VMEM(array.shape, array.dtype) for array in staged]
        + [
            pltpu.VMEM((128, 2048), f32),
            pltpu.VMEM((128, 2048), bf16),
            pltpu.VMEM((128, 2048), f32),
            pltpu.VMEM((2048, 128), f32),
            pltpu.VMEM((1536, 128), bf16),
            pltpu.VMEM((1024, 128), bf16),
            pltpu.VMEM((128, 512), bf16),
        ]
        + [pltpu.VMEM((2, 128, 32, 128), bf16)] * 2
        + [pltpu.VMEM((4096, 128), f32)]
        + [pltpu.VMEM((2, 128, 16, 128), bf16)] * 2
        + [pltpu.VMEM((512, 512), bf16)] * 3
        + [
            pltpu.VMEM((2, 64, 128), bf16),
            pltpu.VMEM((2, 64, 128), bf16),
            pltpu.VMEM((16, 128), f32),
            pltpu.VMEM((2, 8, 128), jnp.int32),
            pltpu.VMEM((8, 128), jnp.int32),
            pltpu.VMEM((WIDE, 128), bf16),
            pltpu.VMEM((SLOTS, 128), f32),
            pltpu.VMEM((2, 128, 512), bf16),
            pltpu.VMEM((64, 16, 128), bf16),
            pltpu.VMEM((64, 16, 128), bf16),
            pltpu.VMEM((16, 128), f32),
            pltpu.VMEM((8, 16, 128), f32),
            pltpu.VMEM((16, 8, 128), f32),
            pltpu.VMEM((256, 2048), bf16),
            pltpu.VMEM((32, 128), f32),
            pltpu.VMEM((32, 128), bf16),
            pltpu.VMEM((16, 32, 128), bf16),
            pltpu.SemaphoreType.DMA((14,)),
            pltpu.SemaphoreType.DMA((14,)),
            pltpu.SemaphoreType.REGULAR,
            pltpu.SemaphoreType.DMA((11,)),
        ],
        compiler_params=pltpu.CompilerParams(
            collective_id=0, has_side_effects=True, vmem_limit_bytes=60 * 1024 * 1024
        ),
        name="atoms_and_pair",
    )(atom_token.reshape(1, SLOTS), atom_mask.reshape(1, SLOTS), *staged)

    def hand_over(pair_ref, atoms_ref, pair_to, atoms_to, pair_held, atoms_held, loaded, stored):
        parts = [(pair_ref.at[pl.ds(k * 8, 8)], pair_held.at[pl.ds(k * 8, 8)], pair_to.at[pl.ds(k * 8, 8)])
                 for k in range(4)] + [(atoms_ref, atoms_held, atoms_to)]
        loads = [pltpu.make_async_copy(a, b, loaded.at[k]) for k, (a, b, _) in enumerate(parts)]
        stores = [pltpu.make_async_copy(b, c, stored.at[k]) for k, (_, b, c) in enumerate(parts)]
        for load in loads:
            load.start()
        for load, store in zip(loads, stores):
            load.wait()
            store.start()
        for store in stores:
            store.wait()

    hbm = pl.BlockSpec(memory_space=pl.ANY)
    return pl.pallas_call(
        hand_over,
        out_shape=(
            jax.ShapeDtypeStruct(pair_in.shape, bf16),
            jax.ShapeDtypeStruct(atoms_in.shape, bf16),
        ),
        in_specs=[hbm] * 2,
        out_specs=(hbm, hbm),
        scratch_shapes=[
            pltpu.VMEM(pair_in.shape, bf16),
            pltpu.VMEM(atoms_in.shape, bf16),
            pltpu.SemaphoreType.DMA((5,)),
            pltpu.SemaphoreType.DMA((5,)),
        ],
        compiler_params=pltpu.CompilerParams(vmem_limit_bytes=60 * 1024 * 1024),
        name="hand_over",
    )(pair_out, atoms_out)


def solution(mesh):
    placed = (
        P("row", "col", None),
        P(("row", "col"), None),
        P(("row", "col")),
        P(("row", "col")),
        P(),
        P(),
        P(),
        P(),
        P(),
        P(),
        P(),
        P(),
        P(),
    )
    return jax.shard_map(
        body,
        mesh=mesh,
        in_specs=placed,
        out_specs=(P("row", "col", None), P(("row", "col"), None)),
        check_vma=False,
    )
```
